32 devices in a mesh: grp: 4 (over z), tile: 4 (over y, core), rep: 2 (over x).
Axes of the slice: x: 2, y: 2, z: 4, core: 2. Of those that a mesh axis runs over, the one named last changes fastest.
Arguments:
- amplitudes: bfloat16 [64, 8, 4096], P(('grp', 'tile')), may hold values from -6 to 6
- tile_blocks: int32 [64, 2], P(('grp', 'tile')), may hold values from 0 to 63, as said below
- live_rows: int32 [64], P(('grp', 'tile')), may hold values from 4 to 8
- ladder_factors: bfloat16 [32, 2, 32, 4096], P('tile', None, 'rep'), may hold values from -0.3125 to 0.3125
- cycle_coupling: bfloat16 [64, 8, 8], replicated, may hold values from -2 to 2
- block_owner: int32 [32], replicated, may hold values from 0 to 31, as said below
Outputs:
- residual: bfloat16 [64, 8, 4096], P(('grp', 'tile'), 'rep')
The draws below stay inside these ranges and needn't reach their ends.
Inputs may be any that keep to these rules, and one draw needn't show every extreme that they name: Column 0 is an occupied-pair block below 64, column 1 a virtual-pair block below 32. Among the tiles of one index pair of grp and tile, at most 2 have blocks whose owner position block_owner[tile_blocks[k, 1]] // 8 is the same; in every group of grp some owner has exactly 2 from every index of tile. `block_owner`: A permutation of the virtual-pair blocks.
All inputs are finite; a program needn't handle non-finite values.
Results may differ from the reference program's by a relative error of at most 0.0036.
Values may be sent and summed in bfloat16 or wider, within the bound.
A program may use at most 64 MiB of HBM per device.

```python
import jax
import jax.numpy as jnp
from jax import lax

VB = 64
VV = 4096
NQ = 32
OP = 8
CAP = 2
TD = 4
VB_DEV = 8
NVB = 32
NOB = 64
TILES = 64
N_TILE = 4


def owner_inverse(key):
    return jax.random.permutation(key, NVB)


def draw_block_owner(key, part):
    inverse = owner_inverse(key)
    return jnp.argsort(inverse).astype(jnp.int32)


def draw_tile_blocks(key, part):
    inverse = owner_inverse(key)
    key = jax.random.fold_in(key, 23)
    sources = TILES // TD
    groups = TILES // (TD * N_TILE)
    key_hot, key_src = jax.random.split(key)
    hottest = jax.random.randint(key_hot, (groups,), 0, N_TILE)
    per_source = hottest[jnp.arange(sources) // N_TILE]
    keys = jax.random.split(key_src, sources)

    def one_source(sub, heavy):
        first, second, third, fourth = jax.random.split(sub, 4)
        others = jax.random.permutation(first, (N_TILE - 1) * CAP)[:TD - CAP]
        target_rest = (heavy + 1 + others // CAP) % N_TILE
        target = jnp.concatenate([jnp.full((CAP,), heavy, jnp.int32), target_rest.astype(jnp.int32)])
        inside = jax.random.randint(second, (TD,), 0, VB_DEV)
        virtual = inverse[target * VB_DEV + inside]
        occupied = jax.random.randint(third, (TD,), 0, NOB)
        order = jax.random.permutation(fourth, TD)
        return jnp.stack([occupied[order], virtual[order]], axis=1).astype(jnp.int32)
    blocks = jax.vmap(one_source)(keys, per_source)
    return blocks.reshape(TILES, 2).astype(jnp.int32)


def touch_ends(drawn, key, smallest, largest):
    spot = [jax.random.randint(jax.random.fold_in(key, axis), (), 0, length) for axis, length in enumerate(drawn.shape)]
    longest = drawn.shape.index(max(drawn.shape))
    next_to = spot[:longest] + [(spot[longest] + 1) % drawn.shape[longest]] + spot[longest + 1:]
    return drawn.at[tuple(spot)].set(smallest).at[tuple(next_to)].set(largest)


def block_levels(own_key, shape, shards, smallest, high):
    level = 1.0
    for position, blocks in shards:
        draws = jax.random.uniform(jax.random.fold_in(jax.random.fold_in(own_key, 6), position), (blocks,), jnp.float32, smallest / len(shards), high / len(shards))
        level = level * jnp.repeat(jnp.exp(draws), shape[position] // blocks).reshape((-1,) + (1,) * (len(shape) - 1 - position))
    return level


def normal_values(stream_key, extent, scale, reach, pieces=(), dtype=jnp.bfloat16):
    drawn = scale * jax.random.normal(stream_key, extent, jnp.float32)
    if pieces:
        drawn = drawn * block_levels(stream_key, extent, pieces, -0.22, 0.18)
    return jnp.clip(drawn, -reach, reach).astype(dtype)


def setup_inputs(seed: int = 0) -> dict:
    key_list = jax.random.split(jax.random.key(seed), 7)
    return {
        "amplitudes": normal_values(key_list[0], (TILES, OP, VV), 1.0, 6.0, ((0, 16),)),
        "tile_blocks": draw_tile_blocks(jax.random.fold_in(key_list[6], 71), 0),
        "live_rows": touch_ends(jax.random.randint(key_list[2], (TILES,), OP // 2, OP + 1), jax.random.fold_in(key_list[2], 1), OP // 2, OP).astype(jnp.int32),
        "ladder_factors": normal_values(key_list[3], (NVB, 2, NQ, VV), (VB * 6) ** -0.5, 0.3125, ((0, 4), (2, 2))),
        "cycle_coupling": normal_values(key_list[4], (NOB, OP, OP), OP ** -0.5, 2.0),
        "block_owner": draw_block_owner(jax.random.fold_in(key_list[6], 71), 0),
    }


def ladder_batch(grid, factor):
    count = grid.shape[0]
    cells = grid.reshape(count, OP, VB, VB).astype(jnp.float32)
    blocks = factor.reshape(count, 2, NQ, VB, VB).astype(jnp.float32)
    middle = jnp.einsum('kqac,kpcd->kpqad', blocks[:, 0], cells).astype(jnp.bfloat16)
    middle = lax.optimization_barrier(middle).astype(jnp.float32)
    ladder = jnp.einsum('kpqad,kqbd->kpab', middle, blocks[:, 1])
    return ladder.reshape(count, OP, VV)


def reference(amplitudes, tile_blocks, live_rows, ladder_factors, cycle_coupling, block_owner):
    live = jnp.arange(OP)[None, :] < live_rows[:, None]
    masked = jnp.where(live[:, :, None], amplitudes, jnp.zeros_like(amplitudes)).astype(jnp.bfloat16)
    place = block_owner[tile_blocks[:, 1]].astype(jnp.int32)
    coupling = cycle_coupling[tile_blocks[:, 0]].astype(jnp.float32)
    batches = TILES // TD

    def one_batch(pair):
        grid, where, mix = pair
        factor = jnp.take(ladder_factors, where, axis=0)
        cycle = jnp.einsum('kpq,kqx->kpx', mix, grid.astype(jnp.float32))
        return (ladder_batch(grid, factor) + cycle).astype(jnp.bfloat16)

    result = lax.map(one_batch, (masked.reshape(batches, TD, OP, VV), place.reshape(batches, TD), coupling.reshape(batches, TD, OP, OP)))
    return result.reshape(TILES, OP, VV)
```

```python
import functools

import jax
import jax.numpy as jnp
from jax import lax
from jax.experimental import pallas as pl
from jax.experimental.pallas import tpu as pltpu
from jax.sharding import PartitionSpec as P

VB = 64
CAP = 2
LANES = 128
HALF = VB // 2
QG = 4
MESH = pl.DeviceIdType.MESH


def low_half(rows):
    return lax.broadcasted_iota(jnp.int32, (rows, LANES), 1) < VB


def swap(value):
    return pltpu.roll(value, VB, 1)


def pair_rows(first, second):
    low = low_half(first.shape[0])
    even = jnp.where(low, first, swap(second))
    odd = jnp.where(low, swap(first), second)
    return even, odd


def spread_rows(value, wide):
    n = value.shape[0]
    for j in range(HALF):
        wide[pl.ds(j * n, n), :] = value[:, j * LANES:(j + 1) * LANES]


def kernel(
    peers, reps, tiles, depth, share, rows,
    blocks_ref, live_ref, owner_ref, amp_ref, coup_ref, fac_hbm,
    out_ref,
    fac, wide, cwide, ctile, packed, xs, xr, tag_send, tag_recv, tag_smem,
    left, right, weight, mid, result, kept, rs_send, rs_recv, back, ret, cyc,
    fac_sem, tag_local, tag_ssem, tag_rsem, x_ssem, x_rsem, rs_ssem, rs_rsem, b_ssem, b_rsem,
):
    groups = depth // QG
    chips = peers // 2
    slots = peers * CAP
    owned = fac_hbm.shape[0]
    me = lax.axis_index("tile")
    my_rep = lax.axis_index("rep")
    my_chip, my_core = me // 2, me % 2

    def to_peer(o):
        return (my_chip + o // 2) % chips * 2 + (my_core + o % 2) % 2

    def from_peer(o):
        return (my_chip + chips - o // 2) % chips * 2 + (my_core + o % 2) % 2

    def rep_peer(i):
        return (my_rep + i) % reps

    factors_copy = pltpu.make_async_copy(fac_hbm, fac, fac_sem)
    factors_copy.start()

    barrier = pltpu.get_barrier_semaphore()

    @pl.loop(1, peers)
    def _(o):
        pl.semaphore_signal(barrier, inc=1, device_id={"tile": to_peer(o)}, device_id_type=MESH)

    for i in range(1, reps):
        pl.semaphore_signal(barrier, inc=1, device_id={"rep": rep_peer(i)}, device_id_type=MESH)

    target, within, slot = [], [], []
    for k in range(tiles):
        place = owner_ref[blocks_ref[k, 1]]
        t = place // owned
        rank = 0
        for e in range(k):
            rank = rank + jnp.where(target[e] == t, 1, 0)
        m = (t // 2 + chips - my_chip) % chips
        c = (t % 2 + 2 - my_core) % 2
        target.append(t)
        within.append(place - t * owned)
        slot.append((m * 2 + c) * CAP + jnp.minimum(rank, CAP - 1))

    @pl.loop(0, tiles)
    def _(k):
        live = live_ref[k]
        row = lax.broadcasted_iota(jnp.int32, (rows, VB * VB), 0)
        masked = jnp.where(row < live, amp_ref[k].astype(jnp.float32), 0.0)
        spread_rows(masked, wide)
        for pair in range(rows // 2):
            first = wide[pl.ds(2 * pair, HALF, stride=rows), :]
            second = wide[pl.ds(2 * pair + 1, HALF, stride=rows), :]
            even, odd = pair_rows(first, second)
            ctile[pl.ds(pair * VB, HALF, stride=2), :] = even
            ctile[pl.ds(pair * VB + 1, HALF, stride=2), :] = odd
        packed[k] = ctile[...].astype(jnp.bfloat16)

    @pl.loop(0, peers)
    def _(o):
        tags = jnp.zeros((8, LANES), jnp.int32)
        row = lax.broadcasted_iota(jnp.int32, (8, LANES), 0)
        for j in range(CAP):
            s = o * CAP + j
            pick, tag = 0, 0
            for k in range(tiles):
                hit = slot[k] == s
                pick = jnp.where(hit, k, pick)
                tag = jnp.where(hit, within[k], tag)
            tags = jnp.where(row == j, tag, tags)
            xs[s] = packed[pick]
        tag_send[o] = tags

    pl.semaphore_wait(barrier, peers - 1 + reps - 1)

    def tag_copy(o):
        return pltpu.make_async_remote_copy(
            src_ref=tag_send.at[o], dst_ref=tag_recv.at[o], send_sem=tag_ssem.at[o], recv_sem=tag_rsem.at[o],
            device_id={"tile": to_peer(o)}, device_id_type=MESH)

    def x_copy(s):
        return pltpu.make_async_remote_copy(
            src_ref=xs.at[s], dst_ref=xr.at[s], send_sem=x_ssem.at[s], recv_sem=x_rsem.at[s],
            device_id={"tile": to_peer(s // CAP)}, device_id_type=MESH)

    def rs_copy(s, i):
        return pltpu.make_async_remote_copy(
            src_ref=rs_send.at[s, i - 1], dst_ref=rs_recv.at[s, i - 1],
            send_sem=rs_ssem.at[s, i - 1], recv_sem=rs_rsem.at[s, i - 1],
            device_id={"rep": rep_peer(i)}, device_id_type=MESH)

    def back_copy(s):
        return pltpu.make_async_remote_copy(
            src_ref=back.at[s], dst_ref=ret.at[s], send_sem=b_ssem.at[s], recv_sem=b_rsem.at[s],
            device_id={"tile": from_peer(s // CAP)}, device_id_type=MESH)

    def to_smem(o, source):
        return pltpu.make_async_copy(source.at[o], tag_smem.at[o], tag_local.at[o])

    @pl.loop(1, peers)
    def _(o):
        tag_copy(o).start()

    @pl.loop(CAP, slots)
    def _(s):
        x_copy(s).start()

    to_smem(0, tag_send).start()

    @pl.loop(0, tiles)
    def _(k):
        live = live_ref[k]
        row = lax.broadcasted_iota(jnp.int32, (rows, VB * VB), 0)
        masked = jnp.where(row < live, amp_ref[k].astype(jnp.float32), 0.0).astype(jnp.bfloat16)
        terms = jnp.dot(coup_ref[blocks_ref[k, 0]], masked, preferred_element_type=jnp.float32)
        for r in range(reps):
            cyc[k, r] = terms[r * share:(r + 1) * share]

    weight[...] = jnp.zeros_like(weight)
    to_smem(0, tag_send).wait()
    factors_copy.wait()

    low = low_half(VB)

    def compute(message, block):
        for pair in range(rows // 2):
            value = message[pl.ds(pair * VB, VB), :].astype(jnp.float32)
            turned = swap(value)
            for e, (a, b) in enumerate(((value, turned), (turned, value))):
                top = jnp.where(low, a, 0.0).astype(jnp.bfloat16)
                bottom = jnp.where(low, 0.0, b).astype(jnp.bfloat16)
                p = 2 * pair + e
                weight[p, 0:VB, 0:LANES] = top
                weight[p, VB:2 * VB, 0:LANES] = bottom
                weight[p, 2 * VB:3 * VB, LANES:] = top
                weight[p, 3 * VB:, LANES:] = bottom
        spread_rows(fac[block, 0].astype(jnp.float32), cwide)
        for pair in range(depth // 2):
            first = cwide[pl.ds(2 * pair, HALF, stride=depth), :]
            second = cwide[pl.ds(2 * pair + 1, HALF, stride=depth), :]
            even, odd = pair_rows(first, second)
            g, h = pair // 2, pair % 2
            left[pl.ds(g * VB, HALF), h * LANES:(h + 1) * LANES] = even.astype(jnp.bfloat16)
            left[pl.ds(g * VB + HALF, HALF), h * LANES:(h + 1) * LANES] = odd.astype(jnp.bfloat16)
        spread_rows(fac[block, 1].astype(jnp.float32), cwide)
        for pair in range(depth // 2):
            first = cwide[pl.ds(2 * pair, HALF, stride=depth), :]
            second = cwide[pl.ds(2 * pair + 1, HALF, stride=depth), :]
            even, odd = pair_rows(first, second)
            ctile[pl.ds(0, HALF, stride=2), :] = even
            ctile[pl.ds(1, HALF, stride=2), :] = odd
            value = ctile[pl.ds(0, VB), :].astype(jnp.bfloat16)
            g, h = pair // 2, pair % 2
            right[g, 0:VB, h * LANES:(h + 1) * LANES] = value
            right[g, VB:, h * LANES:(h + 1) * LANES] = value
        for p in range(rows):
            part = jnp.dot(left[...], weight[p], preferred_element_type=jnp.float32).astype(jnp.bfloat16)
            for g in range(groups):
                mid[g, pl.ds(p * VB, VB), :] = part[g * VB:(g + 1) * VB]
        total = jnp.zeros((rows * VB, LANES), jnp.float32)
        for g in range(groups):
            total = total + lax.dot_general(
                mid[g], right[g], (((1,), (1,)), ((), ())), preferred_element_type=jnp.float32)
        total = total.reshape(rows, 2, HALF, LANES)
        result[...] = jnp.where(low_half(HALF)[None], total[:, 0], total[:, 1])

    def after(s):
        kept[s] = result[pl.ds(my_rep * share, share)].reshape(share * HALF, LANES)
        for i in range(1, reps):
            part = result[pl.ds(rep_peer(i) * share, share)].reshape(share * HALF, LANES)
            rs_send[s, i - 1] = part.astype(jnp.bfloat16)
            rs_copy(s, i).start()

    def summed(s):
        total = kept[s]
        for i in range(1, reps):
            rs_copy(s, i).wait_recv()
            total = total + rs_recv[s, i - 1].astype(jnp.float32)
        return total.astype(jnp.bfloat16)

    def finish(s):
        back[s] = summed(s)
        back_copy(s).start()

    for j in range(CAP):
        xr[j] = xs[j]

    @pl.loop(0, slots)
    def _(s):
        o = s // CAP

        @pl.when(s >= CAP)
        def _():
            x_copy(s).wait_recv()

            @pl.when(s % CAP == 0)
            def _():
                tag_copy(o).wait_recv()
                fetch = to_smem(o, tag_recv)
                fetch.start()
                fetch.wait()

        compute(xr.at[s], tag_smem[o, s % CAP, 0])
        after(s)

        @pl.when(s > CAP)
        def _():
            finish(s - 1)

    for j in range(CAP):
        ret[j] = summed(j)
    finish(slots - 1)

    @pl.loop(CAP, slots)
    def _(s):
        back_copy(s).wait_recv()

    for k in range(tiles):
        wide[pl.ds(0, share * HALF), :] = ret[slot[k]].astype(jnp.float32)
        mine = cyc[k, my_rep]
        for j in range(HALF):
            part = wide[pl.ds(j, share, stride=HALF), :] + mine[:, j * LANES:(j + 1) * LANES]
            out_ref[k, :, j * LANES:(j + 1) * LANES] = part.astype(out_ref.dtype)

    @pl.loop(1, peers)
    def _(o):
        tag_copy(o).wait_send()

    @pl.loop(CAP, slots)
    def _(s):
        x_copy(s).wait_send()
        back_copy(s).wait_send()

    @pl.loop(0, slots)
    def _(s):
        for i in range(1, reps):
            rs_copy(s, i).wait_send()


def solution(mesh):
    peers, reps = mesh.shape["tile"], mesh.shape["rep"]

    def local(amplitudes, tile_blocks, live_rows, ladder_factors, cycle_coupling, block_owner):
        tiles, rows, cells = amplitudes.shape
        owned, _, depth, _ = ladder_factors.shape
        share = rows // reps
        slots = peers * CAP
        groups = depth // QG
        bf16, f32, dma = jnp.bfloat16, jnp.float32, pltpu.SemaphoreType.DMA
        smem, vmem = pltpu.SMEM, pltpu.VMEM
        return pl.pallas_call(
            functools.partial(kernel, peers, reps, tiles, depth, share, rows),
            out_shape=jax.ShapeDtypeStruct((tiles, share, cells), bf16),
            in_specs=[pl.BlockSpec(memory_space=smem)] * 3
            + [pl.BlockSpec(memory_space=vmem)] * 2
            + [pl.BlockSpec(memory_space=pl.ANY)],
            out_specs=pl.BlockSpec(memory_space=vmem),
            scratch_shapes=[
                vmem((owned, 2, depth, cells), bf16),
                vmem((rows * HALF, LANES), f32),
                vmem((depth * HALF, LANES), f32),
                vmem((rows // 2 * VB, LANES), f32),
                vmem((tiles, rows // 2 * VB, LANES), bf16),
                vmem((slots, rows // 2 * VB, LANES), bf16),
                vmem((slots, rows // 2 * VB, LANES), bf16),
                vmem((peers, 8, LANES), jnp.int32),
                vmem((peers, 8, LANES), jnp.int32),
                smem((peers, 8, LANES), jnp.int32),
                vmem((groups * VB, QG * VB), bf16),
                vmem((groups, LANES, QG * VB), bf16),
                vmem((rows, QG * VB, QG * VB), bf16),
                vmem((groups, rows * VB, QG * VB), bf16),
                vmem((rows, HALF, LANES), f32),
                vmem((slots, share * HALF, LANES), f32),
                vmem((slots, reps - 1, share * HALF, LANES), bf16),
                vmem((slots, reps - 1, share * HALF, LANES), bf16),
                vmem((slots, share * HALF, LANES), bf16),
                vmem((slots, share * HALF, LANES), bf16),
                vmem((tiles, reps, share, cells), f32),
                dma,
                dma((peers,)),
                dma((peers,)),
                dma((peers,)),
                dma((slots,)),
                dma((slots,)),
                dma((slots, reps - 1)),
                dma((slots, reps - 1)),
                dma((slots,)),
                dma((slots,)),
            ],
            compiler_params=pltpu.CompilerParams(
                collective_id=0, has_side_effects=True, vmem_limit_bytes=48 * 2**20
            ),
            name="ladder",
        )(tile_blocks, live_rows, block_owner, amplitudes, cycle_coupling, ladder_factors)

    placed = (
        P(("grp", "tile"), None, None),
        P(("grp", "tile"), None),
        P(("grp", "tile")),
        P("tile", None, "rep", None),
        P(),
        P(),
    )
    return jax.shard_map(
        local,
        mesh=mesh,
        in_specs=placed,
        out_specs=P(("grp", "tile"), "rep", None),
        check_vma=False,
    )
```

```python
import functools

import jax
import jax.numpy as jnp
from jax import lax
from jax.experimental import pallas as pl
from jax.experimental.pallas import tpu as pltpu
from jax.sharding import PartitionSpec as P

VB = 64
CAP = 2
LANES = 128
HALF = VB // 2
QG = 4
MESH = pl.DeviceIdType.MESH


def low_half(rows):
    return lax.broadcasted_iota(jnp.int32, (rows, LANES), 1) < VB


def swap(value):
    return pltpu.roll(value, VB, 1)


def pair_rows(first, second):
    low = low_half(first.shape[0])
    even = jnp.where(low, first, swap(second))
    odd = jnp.where(low, swap(first), second)
    return even, odd


def spread_rows(value, wide):
    n = value.shape[0]
    for j in range(HALF):
        wide[pl.ds(j * n, n), :] = value[:, j * LANES:(j + 1) * LANES]


def kernel(
    peers, reps, tiles, depth, share, rows,
    blocks_hbm, live_hbm, owner_hbm, amp_hbm, coup_hbm, fac_hbm,
    out_ref,
    blocks_ref, live_ref, owner_ref, amp_ref, coup_ref, fac, wide, cwide, ctile, packed, xs, xr,
    tag_send, tag_recv, tag_smem, left, right, weight, mid, kept, rs_send, rs_recv, back, ret, cyc,
    in_sem, tag_local, tag_ssem, tag_rsem, x_ssem, x_rsem, rs_ssem, rs_rsem, b_ssem, b_rsem,
):
    groups = depth // QG
    chips = peers // 2
    slots = peers * CAP
    steps = slots // 2
    owned = fac_hbm.shape[0]
    me = lax.axis_index("tile")
    my_rep = lax.axis_index("rep")
    my_chip, my_core = me // 2, me % 2

    def to_peer(o):
        return (my_chip + o // 2) % chips * 2 + (my_core + o % 2) % 2

    def from_peer(o):
        return (my_chip + chips - o // 2) % chips * 2 + (my_core + o % 2) % 2

    def rep_peer(i):
        return (my_rep + i) % reps

    loads = [
        pltpu.make_async_copy(source, target, in_sem.at[n])
        for n, (source, target) in enumerate((
            (amp_hbm, amp_ref), (blocks_hbm, blocks_ref), (live_hbm, live_ref),
            (owner_hbm, owner_ref), (coup_hbm, coup_ref), (fac_hbm, fac)))
    ]
    for load in loads:
        load.start()

    barrier = pltpu.get_barrier_semaphore()

    @pl.loop(1, peers)
    def _(o):
        pl.semaphore_signal(barrier, inc=1, device_id={"tile": to_peer(o)}, device_id_type=MESH)

    for i in range(1, reps):
        pl.semaphore_signal(barrier, inc=1, device_id={"rep": rep_peer(i)}, device_id_type=MESH)

    for load in loads[1:4]:
        load.wait()

    target, within, slot = [], [], []
    for k in range(tiles):
        place = owner_ref[blocks_ref[1, k]]
        t = place // owned
        rank = 0
        for e in range(k):
            rank = rank + jnp.where(target[e] == t, 1, 0)
        m = (t // 2 + chips - my_chip) % chips
        c = (t % 2 + 2 - my_core) % 2
        target.append(t)
        within.append(place - t * owned)
        slot.append((m * 2 + c) * CAP + jnp.minimum(rank, CAP - 1))

    def in_slot(s):
        pick, tag = 0, 0
        for k in range(tiles):
            hit = slot[k] == s
            pick = jnp.where(hit, k, pick)
            tag = jnp.where(hit, within[k], tag)
        return pick, tag

    loads[0].wait()

    @pl.loop(0, tiles)
    def _(k):
        live = live_ref[k]
        row = lax.broadcasted_iota(jnp.int32, (rows, VB * VB), 0)
        masked = jnp.where(row < live, amp_ref[k].astype(jnp.float32), 0.0)
        spread_rows(masked, wide)
        for pair in range(rows // 2):
            first = wide[pl.ds(2 * pair, HALF, stride=rows), :]
            second = wide[pl.ds(2 * pair + 1, HALF, stride=rows), :]
            even, odd = pair_rows(first, second)
            ctile[pl.ds(pair * VB, HALF, stride=2), :] = even
            ctile[pl.ds(pair * VB + 1, HALF, stride=2), :] = odd
        packed[k] = ctile[...].astype(jnp.bfloat16)

    own_tags = []
    for j in range(CAP):
        pick, tag = in_slot(j)
        xr[j] = packed[pick]
        own_tags.append(tag)

    @pl.loop(1, peers)
    def _(o):
        tags = jnp.zeros((8, LANES), jnp.int32)
        row = lax.broadcasted_iota(jnp.int32, (8, LANES), 0)
        for j in range(CAP):
            pick, tag = in_slot(o * CAP + j)
            tags = jnp.where(row == j, tag, tags)
            xs[o * CAP + j] = packed[pick]
        tag_send[o] = tags

    pl.semaphore_wait(barrier, peers - 1 + reps - 1)

    def tag_copy(o):
        return pltpu.make_async_remote_copy(
            src_ref=tag_send.at[o], dst_ref=tag_recv.at[o], send_sem=tag_ssem.at[o], recv_sem=tag_rsem.at[o],
            device_id={"tile": to_peer(o)}, device_id_type=MESH)

    def x_copy(s):
        return pltpu.make_async_remote_copy(
            src_ref=xs.at[s], dst_ref=xr.at[s], send_sem=x_ssem.at[s], recv_sem=x_rsem.at[s],
            device_id={"tile": to_peer(s // CAP)}, device_id_type=MESH)

    def rs_copy(s, i):
        return pltpu.make_async_remote_copy(
            src_ref=rs_send.at[s, i - 1], dst_ref=rs_recv.at[s, i - 1],
            send_sem=rs_ssem.at[s, i - 1], recv_sem=rs_rsem.at[s, i - 1],
            device_id={"rep": rep_peer(i)}, device_id_type=MESH)

    def back_copy(s):
        return pltpu.make_async_remote_copy(
            src_ref=back.at[s], dst_ref=ret.at[s], send_sem=b_ssem.at[s], recv_sem=b_rsem.at[s],
            device_id={"tile": from_peer(s // CAP)}, device_id_type=MESH)

    def to_smem(o):
        return pltpu.make_async_copy(tag_recv.at[o], tag_smem.at[o], tag_local.at[o])

    @pl.loop(1, peers)
    def _(o):
        tag_copy(o).start()

    @pl.loop(CAP, slots)
    def _(s):
        x_copy(s).start()

    low = low_half(VB)

    def prepare(b, block):
        spread_rows(fac[block, 0].astype(jnp.float32), cwide.at[2 * b])
        spread_rows(fac[block, 1].astype(jnp.float32), cwide.at[2 * b + 1])
        for pair in range(depth // 2):
            first = cwide[2 * b, pl.ds(2 * pair, HALF, stride=depth), :]
            second = cwide[2 * b, pl.ds(2 * pair + 1, HALF, stride=depth), :]
            even, odd = pair_rows(first, second)
            g, h = pair // 2, pair % 2
            left[b, pl.ds(g * VB, HALF), h * LANES:(h + 1) * LANES] = even.astype(jnp.bfloat16)
            left[b, pl.ds(g * VB + HALF, HALF), h * LANES:(h + 1) * LANES] = odd.astype(jnp.bfloat16)
        for pair in range(depth // 2):
            first = cwide[2 * b + 1, pl.ds(2 * pair, HALF, stride=depth), :]
            second = cwide[2 * b + 1, pl.ds(2 * pair + 1, HALF, stride=depth), :]
            even, odd = pair_rows(first, second)
            ctile[pl.ds(pair % 2 * VB, HALF, stride=2), :] = even
            ctile[pl.ds(pair % 2 * VB + 1, HALF, stride=2), :] = odd
            value = ctile[pl.ds(pair % 2 * VB, VB), :].astype(jnp.bfloat16)
            right[b, 0:VB, pair * LANES:(pair + 1) * LANES] = value
            right[b, VB:, pair * LANES:(pair + 1) * LANES] = value

    def compute(b, s):
        message = xr.at[s]
        for pair in range(rows // 2):
            value = message[pl.ds(pair * VB, VB), :].astype(jnp.float32)
            turned = swap(value)
            for e, (one, two) in enumerate(((value, turned), (turned, value))):
                top = jnp.where(low, one, 0.0).astype(jnp.bfloat16)
                bottom = jnp.where(low, 0.0, two).astype(jnp.bfloat16)
                p = 2 * pair + e
                weight[b, p, 0:VB, 0:LANES] = top
                weight[b, p, VB:2 * VB, 0:LANES] = bottom
                weight[b, p, 2 * VB:3 * VB, LANES:] = top
                weight[b, p, 3 * VB:, LANES:] = bottom
        for p in range(rows):
            part = jnp.dot(left[b], weight[b, p], preferred_element_type=jnp.float32).astype(jnp.bfloat16)
            for g in range(groups):
                mid[b, pl.ds(p * VB, VB), g * QG * VB:(g + 1) * QG * VB] = part[g * VB:(g + 1) * VB]
        total = lax.dot_general(
            mid[b], right[b], (((1,), (1,)), ((), ())), preferred_element_type=jnp.float32)
        total = total.reshape(rows, 2, HALF, LANES)
        total = jnp.where(low_half(HALF)[None], total[:, 0], total[:, 1])
        for r in range(reps):
            kept[s, r] = total[r * share:(r + 1) * share].reshape(share * HALF, LANES)

    def exchange(s):
        for i in range(1, reps):
            rs_send[s, i - 1] = kept[s, rep_peer(i)].astype(jnp.bfloat16)
            rs_copy(s, i).start()

    def summed(s):
        total = kept[s, my_rep]
        for i in range(1, reps):
            rs_copy(s, i).wait_recv()
            total = total + rs_recv[s, i - 1].astype(jnp.float32)
        return total.astype(jnp.bfloat16)

    def finish(s):
        back[s] = summed(s)
        back_copy(s).start()

    loads[4].wait()

    @pl.loop(0, tiles)
    def _(k):
        live = live_ref[k]
        row = lax.broadcasted_iota(jnp.int32, (rows, VB * VB), 0)
        masked = jnp.where(row < live, amp_ref[k].astype(jnp.float32), 0.0).astype(jnp.bfloat16)
        coup = coup_ref[...].astype(jnp.float32)
        chosen = lax.broadcasted_iota(jnp.int32, coup.shape, 2) == blocks_ref[0, k]
        coup = jnp.sum(jnp.where(chosen, coup, 0.0), axis=2).astype(jnp.bfloat16)
        terms = jnp.dot(coup, masked, preferred_element_type=jnp.float32)
        for r in range(reps):
            cyc[k, r] = terms[r * share:(r + 1) * share]

    weight[...] = jnp.zeros_like(weight)
    loads[5].wait()
    prepare(0, own_tags[0])

    @pl.loop(1, peers)
    def _(o):
        tag_copy(o).wait_recv()
        to_smem(o).start()

    @pl.loop(1, peers)
    def _(o):
        to_smem(o).wait()

    @pl.loop(0, steps)
    def _(n):
        s0 = jnp.where(n == 0, 0, 2 * n + 1)
        s1 = jnp.where(n == steps - 1, 1, 2 * n + 2)
        s2 = jnp.where(n == steps - 1, CAP, 2 * n + 3)
        tag1 = jnp.where(n == steps - 1, own_tags[1], tag_smem[jnp.maximum(s1 // CAP, 1), s1 % CAP, 0])
        tag2 = tag_smem[s2 // CAP, s2 % CAP, 0]

        @pl.when(n > 0)
        def _():
            x_copy(s0).wait_recv()

        compute(0, s0)
        prepare(1, tag1)
        exchange(s0)

        @pl.when(n > 0)
        def _():
            finish(2 * n)

        @pl.when(n < steps - 1)
        def _():
            x_copy(s1).wait_recv()

        compute(1, s1)
        prepare(0, tag2)
        exchange(s1)

        @pl.when(n > 0)
        def _():
            finish(s0)

    for j in range(CAP):
        ret[j] = summed(j)

    @pl.loop(CAP, slots)
    def _(s):
        back_copy(s).wait_recv()

    for k in range(tiles):
        wide[pl.ds(0, share * HALF), :] = ret[slot[k]].astype(jnp.float32)
        mine = cyc[k, my_rep]
        for j in range(HALF):
            part = wide[pl.ds(j, share, stride=HALF), :] + mine[:, j * LANES:(j + 1) * LANES]
            out_ref[k, :, j * LANES:(j + 1) * LANES] = part.astype(out_ref.dtype)

    @pl.loop(1, peers)
    def _(o):
        tag_copy(o).wait_send()

    @pl.loop(CAP, slots)
    def _(s):
        x_copy(s).wait_send()
        back_copy(s).wait_send()

    @pl.loop(0, slots)
    def _(s):
        for i in range(1, reps):
            rs_copy(s, i).wait_send()


def solution(mesh):
    peers, reps = mesh.shape["tile"], mesh.shape["rep"]

    def local(amplitudes, tile_blocks, live_rows, ladder_factors, cycle_coupling, block_owner):
        tiles, rows, cells = amplitudes.shape
        owned, _, depth, _ = ladder_factors.shape
        share = rows // reps
        slots = peers * CAP
        groups = depth // QG
        bf16, f32, dma = jnp.bfloat16, jnp.float32, pltpu.SemaphoreType.DMA
        smem, vmem = pltpu.SMEM, pltpu.VMEM
        return pl.pallas_call(
            functools.partial(kernel, peers, reps, tiles, depth, share, rows),
            out_shape=jax.ShapeDtypeStruct((tiles, share, cells), bf16),
            in_specs=[pl.BlockSpec(memory_space=pl.ANY)] * 6,
            out_specs=pl.BlockSpec(memory_space=vmem),
            scratch_shapes=[
                smem(tile_blocks.shape[::-1], jnp.int32),
                smem(live_rows.shape, jnp.int32),
                smem(block_owner.shape, jnp.int32),
                vmem(amplitudes.shape, bf16),
                vmem((rows, rows, cycle_coupling.shape[0]), bf16),
                vmem(ladder_factors.shape, bf16),
                vmem((rows * HALF, LANES), f32),
                vmem((4, depth * HALF, LANES), f32),
                vmem((rows // 2 * VB, LANES), f32),
                vmem((tiles, rows // 2 * VB, LANES), bf16),
                vmem((slots, rows // 2 * VB, LANES), bf16),
                vmem((slots, rows // 2 * VB, LANES), bf16),
                vmem((peers, 8, LANES), jnp.int32),
                vmem((peers, 8, LANES), jnp.int32),
                smem((peers, 8, LANES), jnp.int32),
                vmem((2, groups * VB, QG * VB), bf16),
                vmem((2, LANES, depth * VB), bf16),
                vmem((2, rows, QG * VB, QG * VB), bf16),
                vmem((2, rows * VB, depth * VB), bf16),
                vmem((slots, reps, share * HALF, LANES), f32),
                vmem((slots, reps - 1, share * HALF, LANES), bf16),
                vmem((slots, reps - 1, share * HALF, LANES), bf16),
                vmem((slots, share * HALF, LANES), bf16),
                vmem((slots, share * HALF, LANES), bf16),
                vmem((tiles, reps, share, cells), f32),
                dma((6,)),
                dma((peers,)),
                dma((peers,)),
                dma((peers,)),
                dma((slots,)),
                dma((slots,)),
                dma((slots, reps - 1)),
                dma((slots, reps - 1)),
                dma((slots,)),
                dma((slots,)),
            ],
            compiler_params=pltpu.CompilerParams(
                collective_id=0, has_side_effects=True, vmem_limit_bytes=62 * 2**20
            ),
            name="ladder",
        )(
            tile_blocks.T, live_rows, block_owner, amplitudes,
            jnp.transpose(cycle_coupling, (1, 2, 0)), ladder_factors)

    placed = (
        P(("grp", "tile"), None, None),
        P(("grp", "tile"), None),
        P(("grp", "tile")),
        P("tile", None, "rep", None),
        P(),
        P(),
    )
    return jax.shard_map(
        local,
        mesh=mesh,
        in_specs=placed,
        out_specs=P(("grp", "tile"), "rep", None),
        check_vma=False,
    )
```

```python
import functools

import jax
import jax.numpy as jnp
from jax import lax
from jax.experimental import pallas as pl
from jax.experimental.pallas import tpu as pltpu
from jax.sharding import PartitionSpec as P

VB = 64
CAP = 2
LANES = 128
HALF = VB // 2
MESH = pl.DeviceIdType.MESH


def low_half(rows):
    return lax.broadcasted_iota(jnp.int32, (rows, LANES), 1) < VB


def swap(value):
    return pltpu.roll(value, VB, 1)


def pair_rows(first, second):
    low = low_half(first.shape[0])
    even = jnp.where(low, first, swap(second))
    odd = jnp.where(low, swap(first), second)
    return even, odd


def spread_rows(value, wide):
    n = value.shape[0]
    for j in range(HALF):
        wide[pl.ds(j * n, n), :] = value[:, j * LANES:(j + 1) * LANES]


def kernel(
    peers, reps, tiles, depth, share, rows,
    blocks_hbm, live_hbm, owner_hbm, amp_hbm, coup_hbm, fac_hbm,
    out_ref,
    blocks_ref, live_ref, owner_ref, amp_ref, coup_ref, fac, wide, cwide, ctile, packed, xs, xr,
    tag_send, tag_recv, tag_smem, left, right, mid, kept, rs_send, rs_recv, back, ret, cyc,
    in_sem, tag_local, tag_ssem, tag_rsem, x_ssem, x_rsem, rs_ssem, rs_rsem, b_ssem, b_rsem,
):
    chips = peers // 2
    slots = peers * CAP
    steps = slots // 2
    owned = fac_hbm.shape[0]
    me = lax.axis_index("tile")
    my_rep = lax.axis_index("rep")
    my_chip, my_core = me // 2, me % 2

    def to_peer(o):
        return (my_chip + o // 2) % chips * 2 + (my_core + o % 2) % 2

    def from_peer(o):
        return (my_chip + chips - o // 2) % chips * 2 + (my_core + o % 2) % 2

    def rep_peer(i):
        return (my_rep + i) % reps

    loads = [
        pltpu.make_async_copy(source, target, in_sem.at[n])
        for n, (source, target) in enumerate((
            (amp_hbm, amp_ref), (blocks_hbm, blocks_ref), (live_hbm, live_ref),
            (owner_hbm, owner_ref), (coup_hbm, coup_ref), (fac_hbm, fac)))
    ]
    for load in loads:
        load.start()

    barrier = pltpu.get_barrier_semaphore()

    @pl.loop(1, peers)
    def _(o):
        pl.semaphore_signal(barrier, inc=1, device_id={"tile": to_peer(o)}, device_id_type=MESH)

    for i in range(1, reps):
        pl.semaphore_signal(barrier, inc=1, device_id={"rep": rep_peer(i)}, device_id_type=MESH)

    for load in loads[1:4]:
        load.wait()

    target, within, slot = [], [], []
    for k in range(tiles):
        place = owner_ref[blocks_ref[1, k]]
        t = place // owned
        rank = 0
        for e in range(k):
            rank = rank + jnp.where(target[e] == t, 1, 0)
        m = (t // 2 + chips - my_chip) % chips
        c = (t % 2 + 2 - my_core) % 2
        target.append(t)
        within.append(place - t * owned)
        slot.append((m * 2 + c) * CAP + jnp.minimum(rank, CAP - 1))

    def in_slot(s):
        pick, tag = 0, 0
        for k in range(tiles):
            hit = slot[k] == s
            pick = jnp.where(hit, k, pick)
            tag = jnp.where(hit, within[k], tag)
        return pick, tag

    loads[0].wait()

    @pl.loop(0, tiles)
    def _(k):
        live = live_ref[k]
        row = lax.broadcasted_iota(jnp.int32, (rows, VB * VB), 0)
        masked = jnp.where(row < live, amp_ref[k].astype(jnp.float32), 0.0)
        spread_rows(masked, wide)
        for pair in range(rows // 2):
            first = wide[pl.ds(2 * pair, HALF, stride=rows), :]
            second = wide[pl.ds(2 * pair + 1, HALF, stride=rows), :]
            even, odd = pair_rows(first, second)
            ctile[pl.ds(pair * VB, HALF, stride=2), :] = even
            ctile[pl.ds(pair * VB + 1, HALF, stride=2), :] = odd
        packed[k] = ctile[...].astype(jnp.bfloat16)

    own_tags = []
    for j in range(CAP):
        pick, tag = in_slot(j)
        xr[j] = packed[pick]
        own_tags.append(tag)

    @pl.loop(1, peers)
    def _(o):
        tags = jnp.zeros((8, LANES), jnp.int32)
        row = lax.broadcasted_iota(jnp.int32, (8, LANES), 0)
        for j in range(CAP):
            pick, tag = in_slot(o * CAP + j)
            tags = jnp.where(row == j, tag, tags)
            xs[o * CAP + j] = packed[pick]
        tag_send[o] = tags

    pl.semaphore_wait(barrier, peers - 1 + reps - 1)

    def tag_copy(o):
        return pltpu.make_async_remote_copy(
            src_ref=tag_send.at[o], dst_ref=tag_recv.at[o], send_sem=tag_ssem.at[o], recv_sem=tag_rsem.at[o],
            device_id={"tile": to_peer(o)}, device_id_type=MESH)

    def x_copy(s):
        return pltpu.make_async_remote_copy(
            src_ref=xs.at[s], dst_ref=xr.at[s], send_sem=x_ssem.at[s], recv_sem=x_rsem.at[s],
            device_id={"tile": to_peer(s // CAP)}, device_id_type=MESH)

    def rs_copy(s, i):
        return pltpu.make_async_remote_copy(
            src_ref=rs_send.at[s, i - 1], dst_ref=rs_recv.at[s, i - 1],
            send_sem=rs_ssem.at[s, i - 1], recv_sem=rs_rsem.at[s, i - 1],
            device_id={"rep": rep_peer(i)}, device_id_type=MESH)

    def back_copy(s):
        return pltpu.make_async_remote_copy(
            src_ref=back.at[s], dst_ref=ret.at[s], send_sem=b_ssem.at[s], recv_sem=b_rsem.at[s],
            device_id={"tile": from_peer(s // CAP)}, device_id_type=MESH)

    def to_smem(o):
        return pltpu.make_async_copy(tag_recv.at[o], tag_smem.at[o], tag_local.at[o])

    @pl.loop(1, peers)
    def _(o):
        tag_copy(o).start()

    @pl.loop(CAP, slots)
    def _(s):
        x_copy(s).start()

    low = low_half(VB)

    def prepare(b, block):
        def spread():
            spread_rows(fac[block, 0].astype(jnp.float32), cwide.at[2 * b])
            spread_rows(fac[block, 1].astype(jnp.float32), cwide.at[2 * b + 1])

        def both(pair):
            first = cwide[2 * b, pl.ds(2 * pair, HALF, stride=depth), :]
            second = cwide[2 * b, pl.ds(2 * pair + 1, HALF, stride=depth), :]
            even, odd = pair_rows(first, second)
            left[b, pl.ds(pair * VB, HALF), :] = even.astype(jnp.bfloat16)
            left[b, pl.ds(pair * VB + HALF, HALF), :] = odd.astype(jnp.bfloat16)
            first = cwide[2 * b + 1, pl.ds(2 * pair, HALF, stride=depth), :]
            second = cwide[2 * b + 1, pl.ds(2 * pair + 1, HALF, stride=depth), :]
            even, odd = pair_rows(first, second)
            ctile[pl.ds(pair % 4 * VB, HALF, stride=2), :] = even
            ctile[pl.ds(pair % 4 * VB + 1, HALF, stride=2), :] = odd
            value = ctile[pl.ds(pair % 4 * VB, VB), :].astype(jnp.bfloat16)
            right[b, 0:VB, pair * LANES:(pair + 1) * LANES] = value
            right[b, VB:, pair * LANES:(pair + 1) * LANES] = value

        return [spread] + [functools.partial(both, pair) for pair in range(depth // 2)]

    def compute(b, s, beside):
        message = xr.at[s]
        each = -(-len(beside) // (rows // 2))
        for pair in range(rows // 2):
            value = message[pl.ds(pair * VB, VB), :].astype(jnp.float32)
            turned = swap(value)
            top = jnp.concatenate([jnp.where(low, value, 0.0), jnp.where(low, turned, 0.0)], axis=1)
            bottom = jnp.concatenate([jnp.where(low, 0.0, turned), jnp.where(low, 0.0, value)], axis=1)
            weight = jnp.concatenate([top.astype(jnp.bfloat16), bottom.astype(jnp.bfloat16)], axis=0)
            part = jnp.dot(left[b], weight, preferred_element_type=jnp.float32).astype(jnp.bfloat16)
            for g in range(depth // 2):
                for e in range(2):
                    mid[b, pl.ds((2 * pair + e) * VB, VB), g * LANES:(g + 1) * LANES] = (
                        part[g * VB:(g + 1) * VB, e * LANES:(e + 1) * LANES])
            for step in beside[pair * each:(pair + 1) * each]:
                step()
        total = lax.dot_general(
            mid[b], right[b], (((1,), (1,)), ((), ())), preferred_element_type=jnp.float32)
        total = total.reshape(rows, 2, HALF, LANES)
        total = jnp.where(low_half(HALF)[None], total[:, 0], total[:, 1])
        for r in range(reps):
            kept[s, r] = total[r * share:(r + 1) * share].reshape(share * HALF, LANES)

    def exchange(s):
        for i in range(1, reps):
            rs_send[s, i - 1] = kept[s, rep_peer(i)].astype(jnp.bfloat16)
            rs_copy(s, i).start()

    def summed(s):
        total = kept[s, my_rep]
        for i in range(1, reps):
            rs_copy(s, i).wait_recv()
            total = total + rs_recv[s, i - 1].astype(jnp.float32)
        return total.astype(jnp.bfloat16)

    def finish(s):
        back[s] = summed(s)
        back_copy(s).start()

    loads[4].wait()

    @pl.loop(0, tiles)
    def _(k):
        live = live_ref[k]
        row = lax.broadcasted_iota(jnp.int32, (rows, VB * VB), 0)
        masked = jnp.where(row < live, amp_ref[k].astype(jnp.float32), 0.0).astype(jnp.bfloat16)
        coup = coup_ref[...].astype(jnp.float32)
        chosen = lax.broadcasted_iota(jnp.int32, coup.shape, 2) == blocks_ref[0, k]
        coup = jnp.sum(jnp.where(chosen, coup, 0.0), axis=2).astype(jnp.bfloat16)
        terms = jnp.dot(coup, masked, preferred_element_type=jnp.float32)
        for r in range(reps):
            cyc[k, r] = terms[r * share:(r + 1) * share]

    loads[5].wait()
    for step in prepare(0, own_tags[0]):
        step()

    @pl.loop(1, peers)
    def _(o):
        tag_copy(o).wait_recv()
        to_smem(o).start()

    @pl.loop(1, peers)
    def _(o):
        to_smem(o).wait()

    @pl.loop(0, steps)
    def _(n):
        s0 = jnp.where(n == 0, 0, 2 * n + 1)
        s1 = jnp.where(n == steps - 1, 1, 2 * n + 2)
        s2 = jnp.where(n == steps - 1, CAP, 2 * n + 3)
        tag1 = jnp.where(n == steps - 1, own_tags[1], tag_smem[jnp.maximum(s1 // CAP, 1), s1 % CAP, 0])
        tag2 = tag_smem[s2 // CAP, s2 % CAP, 0]

        @pl.when(n > 0)
        def _():
            x_copy(s0).wait_recv()

        compute(0, s0, prepare(1, tag1))
        exchange(s0)

        @pl.when(n > 0)
        def _():
            finish(2 * n)

        @pl.when(n < steps - 1)
        def _():
            x_copy(s1).wait_recv()

        compute(1, s1, prepare(0, tag2))
        exchange(s1)

        @pl.when(n > 0)
        def _():
            finish(s0)

    for j in range(CAP):
        ret[j] = summed(j)

    @pl.loop(CAP, slots)
    def _(s):
        back_copy(s).wait_recv()

    for k in range(tiles):
        wide[pl.ds(0, share * HALF), :] = ret[slot[k]].astype(jnp.float32)
        mine = cyc[k, my_rep]
        for j in range(HALF):
            part = wide[pl.ds(j, share, stride=HALF), :] + mine[:, j * LANES:(j + 1) * LANES]
            out_ref[k, :, j * LANES:(j + 1) * LANES] = part.astype(out_ref.dtype)

    @pl.loop(1, peers)
    def _(o):
        tag_copy(o).wait_send()

    @pl.loop(CAP, slots)
    def _(s):
        x_copy(s).wait_send()
        back_copy(s).wait_send()

    @pl.loop(0, slots)
    def _(s):
        for i in range(1, reps):
            rs_copy(s, i).wait_send()


def solution(mesh):
    peers, reps = mesh.shape["tile"], mesh.shape["rep"]

    def local(amplitudes, tile_blocks, live_rows, ladder_factors, cycle_coupling, block_owner):
        tiles, rows, cells = amplitudes.shape
        owned, _, depth, _ = ladder_factors.shape
        share = rows // reps
        slots = peers * CAP
        bf16, f32, dma = jnp.bfloat16, jnp.float32, pltpu.SemaphoreType.DMA
        smem, vmem = pltpu.SMEM, pltpu.VMEM
        return pl.pallas_call(
            functools.partial(kernel, peers, reps, tiles, depth, share, rows),
            out_shape=jax.ShapeDtypeStruct((tiles, share, cells), bf16),
            in_specs=[pl.BlockSpec(memory_space=pl.ANY)] * 6,
            out_specs=pl.BlockSpec(memory_space=vmem),
            scratch_shapes=[
                smem(tile_blocks.shape[::-1], jnp.int32),
                smem(live_rows.shape, jnp.int32),
                smem(block_owner.shape, jnp.int32),
                vmem(amplitudes.shape, bf16),
                vmem((rows, rows, cycle_coupling.shape[0]), bf16),
                vmem(ladder_factors.shape, bf16),
                vmem((rows * HALF, LANES), f32),
                vmem((4, depth * HALF, LANES), f32),
                vmem((rows // 2 * VB, LANES), f32),
                vmem((tiles, rows // 2 * VB, LANES), bf16),
                vmem((slots, rows // 2 * VB, LANES), bf16),
                vmem((slots, rows // 2 * VB, LANES), bf16),
                vmem((peers, 8, LANES), jnp.int32),
                vmem((peers, 8, LANES), jnp.int32),
                smem((peers, 8, LANES), jnp.int32),
                vmem((2, depth // 2 * VB, LANES), bf16),
                vmem((2, LANES, depth * VB), bf16),
                vmem((2, rows * VB, depth * VB), bf16),
                vmem((slots, reps, share * HALF, LANES), f32),
                vmem((slots, reps - 1, share * HALF, LANES), bf16),
                vmem((slots, reps - 1, share * HALF, LANES), bf16),
                vmem((slots, share * HALF, LANES), bf16),
                vmem((slots, share * HALF, LANES), bf16),
                vmem((tiles, reps, share, cells), f32),
                dma((6,)),
                dma((peers,)),
                dma((peers,)),
                dma((peers,)),
                dma((slots,)),
                dma((slots,)),
                dma((slots, reps - 1)),
                dma((slots, reps - 1)),
                dma((slots,)),
                dma((slots,)),
            ],
            compiler_params=pltpu.CompilerParams(
                collective_id=0, has_side_effects=True, vmem_limit_bytes=62 * 2**20
            ),
            name="ladder",
        )(
            tile_blocks.T, live_rows, block_owner, amplitudes,
            jnp.transpose(cycle_coupling, (1, 2, 0)), ladder_factors)

    placed = (
        P(("grp", "tile"), None, None),
        P(("grp", "tile"), None),
        P(("grp", "tile")),
        P("tile", None, "rep", None),
        P(),
        P(),
    )
    return jax.shard_map(
        local,
        mesh=mesh,
        in_specs=placed,
        out_specs=P(("grp", "tile"), "rep", None),
        check_vma=False,
    )
```

```python
import functools

import jax
import jax.numpy as jnp
from jax import lax
from jax.experimental import pallas as pl
from jax.experimental.pallas import tpu as pltpu
from jax.sharding import PartitionSpec as P

VB = 64
CAP = 2
LANES = 128
HALF = VB // 2
MESH = pl.DeviceIdType.MESH


def low_half(rows):
    return lax.broadcasted_iota(jnp.int32, (rows, LANES), 1) < VB


def swap(value):
    return pltpu.roll(value, VB, 1)


def pair_rows(first, second):
    low = low_half(first.shape[0])
    even = jnp.where(low, first, swap(second))
    odd = jnp.where(low, swap(first), second)
    return even, odd


def spread_rows(value, wide):
    n = value.shape[0]
    for j in range(HALF):
        wide[pl.ds(j * n, n), :] = value[:, j * LANES:(j + 1) * LANES]


def kernel(
    peers, reps, tiles, depth, share, rows,
    blocks_hbm, live_hbm, owner_hbm, amp_hbm, coup_hbm, fac_hbm,
    out_ref,
    blocks_ref, live_ref, owner_ref, amp_ref, coup_ref, fac, wide, cwide, ctile, packed, xs, xr,
    tag_send, tag_recv, tag_smem, left, right, mid, kept, rs_send, rs_recv, back, ret, cyc,
    in_sem, tag_local, tag_ssem, tag_rsem, x_ssem, x_rsem, relay_ssem, relay_rsem, rs_ssem, rs_rsem, b_ssem, b_rsem,
):
    chips = peers // 2
    slots = peers * CAP
    steps = slots // 2
    near = 2 * CAP
    parts = xs.shape[1:]
    packed_part = (parts[0], parts[1], LANES)
    owned = fac_hbm.shape[0]
    me = lax.axis_index("tile")
    my_rep = lax.axis_index("rep")
    my_chip, my_core = me // 2, me % 2

    def to_peer(o):
        return (my_chip + o // 2) % chips * 2 + (my_core + o % 2) % 2

    def from_peer(o):
        return (my_chip + chips - o // 2) % chips * 2 + (my_core + o % 2) % 2

    def rep_peer(i):
        return (my_rep + i) % reps

    loads = [
        pltpu.make_async_copy(source, target, in_sem.at[n])
        for n, (source, target) in enumerate((
            (amp_hbm, amp_ref), (blocks_hbm, blocks_ref), (live_hbm, live_ref),
            (owner_hbm, owner_ref), (coup_hbm, coup_ref), (fac_hbm, fac)))
    ]
    for load in loads:
        load.start()

    barrier = pltpu.get_barrier_semaphore()

    @pl.loop(1, peers)
    def _(o):
        pl.semaphore_signal(barrier, inc=1, device_id={"tile": to_peer(o)}, device_id_type=MESH)

    for i in range(1, reps):
        pl.semaphore_signal(barrier, inc=1, device_id={"rep": rep_peer(i)}, device_id_type=MESH)

    for load in loads[1:4]:
        load.wait()

    target, within, slot = [], [], []
    for k in range(tiles):
        place = owner_ref[blocks_ref[1, k]]
        t = place // owned
        rank = 0
        for e in range(k):
            rank = rank + jnp.where(target[e] == t, 1, 0)
        m = (t // 2 + chips - my_chip) % chips
        c = (t % 2 + 2 - my_core) % 2
        target.append(t)
        within.append(place - t * owned)
        slot.append((m * 2 + c) * CAP + jnp.minimum(rank, CAP - 1))

    def in_slot(s):
        pick, tag = 0, 0
        for k in range(tiles):
            hit = slot[k] == s
            pick = jnp.where(hit, k, pick)
            tag = jnp.where(hit, within[k], tag)
        return pick, tag

    loads[0].wait()

    @pl.loop(0, tiles)
    def _(k):
        live = live_ref[k]
        row = lax.broadcasted_iota(jnp.int32, (rows, VB * VB), 0)
        masked = jnp.where(row < live, amp_ref[k].astype(jnp.float32), 0.0)
        spread_rows(masked, wide)
        for pair in range(rows // 2):
            first = wide[pl.ds(2 * pair, HALF, stride=rows), :]
            second = wide[pl.ds(2 * pair + 1, HALF, stride=rows), :]
            even, odd = pair_rows(first, second)
            ctile[pl.ds(pair * VB, HALF, stride=2), :] = even
            ctile[pl.ds(pair * VB + 1, HALF, stride=2), :] = odd
        packed[k] = ctile[...].astype(jnp.bfloat16).reshape(packed_part)

    own_tags = []
    for j in range(CAP):
        pick, tag = in_slot(j)
        xr[j] = packed[pick]
        own_tags.append(tag)

    @pl.loop(1, peers)
    def _(o):
        tags = jnp.zeros((8, LANES), jnp.int32)
        row = lax.broadcasted_iota(jnp.int32, (8, LANES), 0)
        for j in range(CAP):
            pick, tag = in_slot(o * CAP + j)
            tags = jnp.where(row == j, tag, tags)
            xs[o * CAP + j] = packed[pick]
        tag_send[o] = tags

    pl.semaphore_wait(barrier, peers - 1 + reps - 1)

    def tag_copy(o):
        return pltpu.make_async_remote_copy(
            src_ref=tag_send.at[o], dst_ref=tag_recv.at[o], send_sem=tag_ssem.at[o], recv_sem=tag_rsem.at[o],
            device_id={"tile": to_peer(o)}, device_id_type=MESH)

    def near_copy(s):
        return pltpu.make_async_remote_copy(
            src_ref=xs.at[s], dst_ref=xr.at[s], send_sem=x_ssem.at[s], recv_sem=x_rsem.at[s],
            device_id={"tile": to_peer(s // CAP)}, device_id_type=MESH)

    def far_copy(s):
        return pltpu.make_async_remote_copy(
            src_ref=xs.at[s, my_rep], dst_ref=xr.at[s, my_rep], send_sem=x_ssem.at[s], recv_sem=x_rsem.at[s],
            device_id={"tile": to_peer(s // CAP)}, device_id_type=MESH)

    def relay_copy(s, i, part):
        return pltpu.make_async_remote_copy(
            src_ref=xr.at[s, part], dst_ref=xr.at[s, part],
            send_sem=relay_ssem.at[s, i - 1], recv_sem=relay_rsem.at[s, i - 1],
            device_id={"rep": rep_peer(i)}, device_id_type=MESH)

    def relay(s):
        far_copy(s).wait_recv()
        for i in range(1, reps):
            relay_copy(s, i, my_rep).start()

    def arrived(s):
        @pl.when(s < near)
        def _():
            near_copy(s).wait_recv()

        @pl.when(s >= near)
        def _():
            for i in range(1, reps):
                relay_copy(s, i, (my_rep + reps - i) % reps).wait_recv()

    def rs_copy(s, i):
        return pltpu.make_async_remote_copy(
            src_ref=rs_send.at[s, i - 1], dst_ref=rs_recv.at[s, i - 1],
            send_sem=rs_ssem.at[s, i - 1], recv_sem=rs_rsem.at[s, i - 1],
            device_id={"rep": rep_peer(i)}, device_id_type=MESH)

    def back_copy(s):
        return pltpu.make_async_remote_copy(
            src_ref=back.at[s], dst_ref=ret.at[s], send_sem=b_ssem.at[s], recv_sem=b_rsem.at[s],
            device_id={"tile": from_peer(s // CAP)}, device_id_type=MESH)

    def to_smem(o):
        return pltpu.make_async_copy(tag_recv.at[o], tag_smem.at[o], tag_local.at[o])

    @pl.loop(1, peers)
    def _(o):
        tag_copy(o).start()

    @pl.loop(near, slots)
    def _(s):
        far_copy(s).start()

    @pl.loop(CAP, near)
    def _(s):
        near_copy(s).start()

    low = low_half(VB)

    def prepare(b, block):
        def spread():
            spread_rows(fac[block, 0].astype(jnp.float32), cwide.at[2 * b])
            spread_rows(fac[block, 1].astype(jnp.float32), cwide.at[2 * b + 1])

        def both(pair):
            first = cwide[2 * b, pl.ds(2 * pair, HALF, stride=depth), :]
            second = cwide[2 * b, pl.ds(2 * pair + 1, HALF, stride=depth), :]
            even, odd = pair_rows(first, second)
            left[b, pl.ds(pair * VB, HALF), :] = even.astype(jnp.bfloat16)
            left[b, pl.ds(pair * VB + HALF, HALF), :] = odd.astype(jnp.bfloat16)
            first = cwide[2 * b + 1, pl.ds(2 * pair, HALF, stride=depth), :]
            second = cwide[2 * b + 1, pl.ds(2 * pair + 1, HALF, stride=depth), :]
            even, odd = pair_rows(first, second)
            ctile[pl.ds(pair % 4 * VB, HALF, stride=2), :] = even
            ctile[pl.ds(pair % 4 * VB + 1, HALF, stride=2), :] = odd
            value = ctile[pl.ds(pair % 4 * VB, VB), :].astype(jnp.bfloat16)
            right[b, 0:VB, pair * LANES:(pair + 1) * LANES] = value
            right[b, VB:, pair * LANES:(pair + 1) * LANES] = value

        return [spread] + [functools.partial(both, pair) for pair in range(depth // 2)]

    def compute(b, s, beside):
        message = xr[s].reshape(rows // 2 * VB, LANES)
        each = -(-len(beside) // (rows // 2))
        for pair in range(rows // 2):
            value = message[pair * VB:(pair + 1) * VB].astype(jnp.float32)
            turned = swap(value)
            top = jnp.concatenate([jnp.where(low, value, 0.0), jnp.where(low, turned, 0.0)], axis=1)
            bottom = jnp.concatenate([jnp.where(low, 0.0, turned), jnp.where(low, 0.0, value)], axis=1)
            weight = jnp.concatenate([top.astype(jnp.bfloat16), bottom.astype(jnp.bfloat16)], axis=0)
            part = jnp.dot(left[b], weight, preferred_element_type=jnp.float32).astype(jnp.bfloat16)
            for g in range(depth // 2):
                for e in range(2):
                    mid[b, pl.ds((2 * pair + e) * VB, VB), g * LANES:(g + 1) * LANES] = (
                        part[g * VB:(g + 1) * VB, e * LANES:(e + 1) * LANES])
            for step in beside[pair * each:(pair + 1) * each]:
                step()
        total = lax.dot_general(
            mid[b], right[b], (((1,), (1,)), ((), ())), preferred_element_type=jnp.float32)
        total = total.reshape(rows, 2, HALF, LANES)
        total = jnp.where(low_half(HALF)[None], total[:, 0], total[:, 1])
        for r in range(reps):
            kept[s, r] = total[r * share:(r + 1) * share].reshape(share * HALF, LANES)

    def exchange(s):
        for i in range(1, reps):
            rs_send[s, i - 1] = kept[s, rep_peer(i)].astype(jnp.bfloat16)
            rs_copy(s, i).start()

    def summed(s):
        total = kept[s, my_rep]
        for i in range(1, reps):
            rs_copy(s, i).wait_recv()
            total = total + rs_recv[s, i - 1].astype(jnp.float32)
        return total.astype(jnp.bfloat16)

    def finish(s):
        back[s] = summed(s)
        back_copy(s).start()

    loads[4].wait()

    @pl.loop(0, tiles)
    def _(k):
        live = live_ref[k]
        row = lax.broadcasted_iota(jnp.int32, (rows, VB * VB), 0)
        masked = jnp.where(row < live, amp_ref[k].astype(jnp.float32), 0.0).astype(jnp.bfloat16)
        coup = coup_ref[...].astype(jnp.float32)
        chosen = lax.broadcasted_iota(jnp.int32, coup.shape, 2) == blocks_ref[0, k]
        coup = jnp.sum(jnp.where(chosen, coup, 0.0), axis=2).astype(jnp.bfloat16)
        terms = jnp.dot(coup, masked, preferred_element_type=jnp.float32)
        for r in range(reps):
            cyc[k, r] = terms[r * share:(r + 1) * share]

    loads[5].wait()
    for step in prepare(0, own_tags[0]):
        step()

    @pl.loop(1, peers)
    def _(o):
        tag_copy(o).wait_recv()
        to_smem(o).start()

    @pl.loop(1, peers)
    def _(o):
        to_smem(o).wait()

    @pl.loop(0, steps)
    def _(n):
        s0 = jnp.where(n == 0, 0, 2 * n + 1)
        s1 = jnp.where(n == steps - 1, 1, 2 * n + 2)
        s2 = jnp.where(n == steps - 1, CAP, 2 * n + 3)
        tag1 = jnp.where(n == steps - 1, own_tags[1], tag_smem[jnp.maximum(s1 // CAP, 1), s1 % CAP, 0])
        tag2 = tag_smem[s2 // CAP, s2 % CAP, 0]

        inner = jnp.logical_and(n > 0, n < steps - 1)

        @pl.when(inner)
        def _():
            relay(s1)

        @pl.when(n > 0)
        def _():
            arrived(s0)

        compute(0, s0, prepare(1, tag1))
        exchange(s0)

        @pl.when(n > 0)
        def _():
            finish(2 * n)

        @pl.when(inner)
        def _():
            relay(2 * n + 3)

        @pl.when(n < steps - 1)
        def _():
            arrived(s1)

        compute(1, s1, prepare(0, tag2))
        exchange(s1)

        @pl.when(n > 0)
        def _():
            finish(s0)

    for j in range(CAP):
        ret[j] = summed(j)

    @pl.loop(CAP, slots)
    def _(s):
        back_copy(s).wait_recv()

    for k in range(tiles):
        wide[pl.ds(0, share * HALF), :] = ret[slot[k]].astype(jnp.float32)
        mine = cyc[k, my_rep]
        for j in range(HALF):
            part = wide[pl.ds(j, share, stride=HALF), :] + mine[:, j * LANES:(j + 1) * LANES]
            out_ref[k, :, j * LANES:(j + 1) * LANES] = part.astype(out_ref.dtype)

    @pl.loop(1, peers)
    def _(o):
        tag_copy(o).wait_send()

    @pl.loop(CAP, near)
    def _(s):
        near_copy(s).wait_send()

    @pl.loop(near, slots)
    def _(s):
        far_copy(s).wait_send()
        for i in range(1, reps):
            relay_copy(s, i, my_rep).wait_send()

    @pl.loop(CAP, slots)
    def _(s):
        back_copy(s).wait_send()

    @pl.loop(0, slots)
    def _(s):
        for i in range(1, reps):
            rs_copy(s, i).wait_send()


def solution(mesh):
    peers, reps = mesh.shape["tile"], mesh.shape["rep"]

    def local(amplitudes, tile_blocks, live_rows, ladder_factors, cycle_coupling, block_owner):
        tiles, rows, cells = amplitudes.shape
        owned, _, depth, _ = ladder_factors.shape
        share = rows // reps
        slots = peers * CAP
        bf16, f32, dma = jnp.bfloat16, jnp.float32, pltpu.SemaphoreType.DMA
        smem, vmem = pltpu.SMEM, pltpu.VMEM
        return pl.pallas_call(
            functools.partial(kernel, peers, reps, tiles, depth, share, rows),
            out_shape=jax.ShapeDtypeStruct((tiles, share, cells), bf16),
            in_specs=[pl.BlockSpec(memory_space=pl.ANY)] * 6,
            out_specs=pl.BlockSpec(memory_space=vmem),
            scratch_shapes=[
                smem(tile_blocks.shape[::-1], jnp.int32),
                smem(live_rows.shape, jnp.int32),
                smem(block_owner.shape, jnp.int32),
                vmem(amplitudes.shape, bf16),
                vmem((rows, rows, cycle_coupling.shape[0]), bf16),
                vmem(ladder_factors.shape, bf16),
                vmem((rows * HALF, LANES), f32),
                vmem((4, depth * HALF, LANES), f32),
                vmem((rows // 2 * VB, LANES), f32),
                vmem((tiles, reps, share // 2 * VB, LANES), bf16),
                vmem((slots, reps, share // 2 * VB, LANES), bf16),
                vmem((slots, reps, share // 2 * VB, LANES), bf16),
                vmem((peers, 8, LANES), jnp.int32),
                vmem((peers, 8, LANES), jnp.int32),
                smem((peers, 8, LANES), jnp.int32),
                vmem((2, depth // 2 * VB, LANES), bf16),
                vmem((2, LANES, depth * VB), bf16),
                vmem((2, rows * VB, depth * VB), bf16),
                vmem((slots, reps, share * HALF, LANES), f32),
                vmem((slots, reps - 1, share * HALF, LANES), bf16),
                vmem((slots, reps - 1, share * HALF, LANES), bf16),
                vmem((slots, share * HALF, LANES), bf16),
                vmem((slots, share * HALF, LANES), bf16),
                vmem((tiles, reps, share, cells), f32),
                dma((6,)),
                dma((peers,)),
                dma((peers,)),
                dma((peers,)),
                dma((slots,)),
                dma((slots,)),
                dma((slots, reps - 1)),
                dma((slots, reps - 1)),
                dma((slots, reps - 1)),
                dma((slots, reps - 1)),
                dma((slots,)),
                dma((slots,)),
            ],
            compiler_params=pltpu.CompilerParams(
                collective_id=0, has_side_effects=True, vmem_limit_bytes=62 * 2**20
            ),
            name="ladder",
        )(
            tile_blocks.T, live_rows, block_owner, amplitudes,
            jnp.transpose(cycle_coupling, (1, 2, 0)), ladder_factors)

    placed = (
        P(("grp", "tile"), None, None),
        P(("grp", "tile"), None),
        P(("grp", "tile")),
        P("tile", None, "rep", None),
        P(),
        P(),
    )
    return jax.shard_map(
        local,
        mesh=mesh,
        in_specs=placed,
        out_specs=P(("grp", "tile"), "rep", None),
        check_vma=False,
    )
```

```python
import functools

import jax
import jax.numpy as jnp
from jax import lax
from jax.experimental import pallas as pl
from jax.experimental.pallas import tpu as pltpu
from jax.sharding import PartitionSpec as P

VB = 64
CAP = 2
LANES = 128
HALF = VB // 2
MESH = pl.DeviceIdType.MESH


def low_half(rows):
    return lax.broadcasted_iota(jnp.int32, (rows, LANES), 1) < VB


def swap(value):
    return pltpu.roll(value, VB, 1)


def pair_rows(first, second):
    low = low_half(first.shape[0])
    even = jnp.where(low, first, swap(second))
    odd = jnp.where(low, swap(first), second)
    return even, odd


def spread_rows(value, wide):
    n = value.shape[0]
    for j in range(HALF):
        wide[pl.ds(j * n, n), :] = value[:, j * LANES:(j + 1) * LANES]


def kernel(
    peers, reps, tiles, depth, share, rows,
    blocks_hbm, live_hbm, owner_hbm, amp_hbm, coup_hbm, fac_hbm,
    out_ref,
    blocks_ref, live_ref, owner_ref, amp_ref, coup_ref, fac, wide, cwide, xtile, ctile, packed, xs, xr,
    tag_send, tag_recv, tag_smem, left, right, mid, kept, rs_send, rs_recv, back, ret, cyc,
    in_sem, tag_local, tag_ssem, tag_rsem, x_ssem, x_rsem, rs_ssem, rs_rsem, b_ssem, b_rsem,
):
    chips = peers // 2
    slots = peers * CAP
    steps = slots // 2
    owned = fac_hbm.shape[0]
    me = lax.axis_index("tile")
    my_rep = lax.axis_index("rep")
    my_chip, my_core = me // 2, me % 2

    def to_peer(o):
        return (my_chip + o // 2) % chips * 2 + (my_core + o % 2) % 2

    def from_peer(o):
        return (my_chip + chips - o // 2) % chips * 2 + (my_core + o % 2) % 2

    def rep_peer(i):
        return (my_rep + i) % reps

    loads = [
        pltpu.make_async_copy(source, target, in_sem.at[n])
        for n, (source, target) in enumerate((
            (amp_hbm, amp_ref), (blocks_hbm, blocks_ref), (live_hbm, live_ref),
            (owner_hbm, owner_ref), (coup_hbm, coup_ref), (fac_hbm, fac)))
    ]
    for load in loads:
        load.start()

    barrier = pltpu.get_barrier_semaphore()

    @pl.loop(1, peers)
    def _(o):
        pl.semaphore_signal(barrier, inc=1, device_id={"tile": to_peer(o)}, device_id_type=MESH)

    for i in range(1, reps):
        pl.semaphore_signal(barrier, inc=1, device_id={"rep": rep_peer(i)}, device_id_type=MESH)

    for load in loads[1:4]:
        load.wait()

    target, within, slot = [], [], []
    for k in range(tiles):
        place = owner_ref[blocks_ref[1, k]]
        t = place // owned
        rank = 0
        for e in range(k):
            rank = rank + jnp.where(target[e] == t, 1, 0)
        m = (t // 2 + chips - my_chip) % chips
        c = (t % 2 + 2 - my_core) % 2
        target.append(t)
        within.append(place - t * owned)
        slot.append((m * 2 + c) * CAP + jnp.minimum(rank, CAP - 1))

    def in_slot(s):
        pick, tag = 0, 0
        for k in range(tiles):
            hit = slot[k] == s
            pick = jnp.where(hit, k, pick)
            tag = jnp.where(hit, within[k], tag)
        return pick, tag

    loads[0].wait()

    row = lax.broadcasted_iota(jnp.int32, (rows, VB * VB), 0)
    for k in range(tiles):
        masked = jnp.where(row < live_ref[k], amp_ref[k].astype(jnp.float32), 0.0)
        spread_rows(masked, wide.at[k])
    for k in range(tiles):
        for pair in range(rows // 2):
            first = wide[k, pl.ds(2 * pair, HALF, stride=rows), :]
            second = wide[k, pl.ds(2 * pair + 1, HALF, stride=rows), :]
            even, odd = pair_rows(first, second)
            xtile[k, pl.ds(pair * VB, HALF, stride=2), :] = even
            xtile[k, pl.ds(pair * VB + 1, HALF, stride=2), :] = odd
    for k in range(tiles):
        packed[k] = xtile[k].astype(jnp.bfloat16)

    own_tags = []
    for j in range(CAP):
        pick, tag = in_slot(j)
        xr[j] = packed[pick]
        own_tags.append(tag)

    @pl.loop(1, peers)
    def _(o):
        tags = jnp.zeros((8, LANES), jnp.int32)
        row = lax.broadcasted_iota(jnp.int32, (8, LANES), 0)
        for j in range(CAP):
            pick, tag = in_slot(o * CAP + j)
            tags = jnp.where(row == j, tag, tags)
            xs[o * CAP + j] = packed[pick]
        tag_send[o] = tags

    pl.semaphore_wait(barrier, peers - 1 + reps - 1)

    def tag_copy(o):
        return pltpu.make_async_remote_copy(
            src_ref=tag_send.at[o], dst_ref=tag_recv.at[o], send_sem=tag_ssem.at[o], recv_sem=tag_rsem.at[o],
            device_id={"tile": to_peer(o)}, device_id_type=MESH)

    def x_copy(s):
        return pltpu.make_async_remote_copy(
            src_ref=xs.at[s], dst_ref=xr.at[s], send_sem=x_ssem.at[s], recv_sem=x_rsem.at[s],
            device_id={"tile": to_peer(s // CAP)}, device_id_type=MESH)

    def rs_copy(s, i):
        return pltpu.make_async_remote_copy(
            src_ref=rs_send.at[s, i - 1], dst_ref=rs_recv.at[s, i - 1],
            send_sem=rs_ssem.at[s, i - 1], recv_sem=rs_rsem.at[s, i - 1],
            device_id={"rep": rep_peer(i)}, device_id_type=MESH)

    def back_copy(s):
        return pltpu.make_async_remote_copy(
            src_ref=back.at[s], dst_ref=ret.at[s], send_sem=b_ssem.at[s], recv_sem=b_rsem.at[s],
            device_id={"tile": from_peer(s // CAP)}, device_id_type=MESH)

    def to_smem(o):
        return pltpu.make_async_copy(tag_recv.at[o], tag_smem.at[o], tag_local.at[o])

    @pl.loop(1, peers)
    def _(o):
        tag_copy(o).start()

    @pl.loop(2 * CAP, slots)
    def _(s):
        x_copy(s).start()

    for s in range(CAP, 2 * CAP):
        x_copy(s).start()

    low = low_half(VB)

    def prepare(b, block):
        def spread():
            spread_rows(fac[block, 0].astype(jnp.float32), cwide.at[2 * b])
            spread_rows(fac[block, 1].astype(jnp.float32), cwide.at[2 * b + 1])

        def both(pair):
            first = cwide[2 * b, pl.ds(2 * pair, HALF, stride=depth), :]
            second = cwide[2 * b, pl.ds(2 * pair + 1, HALF, stride=depth), :]
            even, odd = pair_rows(first, second)
            left[b, pl.ds(pair * VB, HALF), :] = even.astype(jnp.bfloat16)
            left[b, pl.ds(pair * VB + HALF, HALF), :] = odd.astype(jnp.bfloat16)
            first = cwide[2 * b + 1, pl.ds(2 * pair, HALF, stride=depth), :]
            second = cwide[2 * b + 1, pl.ds(2 * pair + 1, HALF, stride=depth), :]
            even, odd = pair_rows(first, second)
            ctile[pl.ds(pair % 4 * VB, HALF, stride=2), :] = even
            ctile[pl.ds(pair % 4 * VB + 1, HALF, stride=2), :] = odd
            value = ctile[pl.ds(pair % 4 * VB, VB), :].astype(jnp.bfloat16)
            right[b, 0:VB, pair * LANES:(pair + 1) * LANES] = value
            right[b, VB:, pair * LANES:(pair + 1) * LANES] = value

        return [spread] + [functools.partial(both, pair) for pair in range(depth // 2)]

    def compute(b, s, beside):
        message = xr.at[s]
        each = -(-len(beside) // (rows // 2))
        for pair in range(rows // 2):
            value = message[pl.ds(pair * VB, VB), :].astype(jnp.float32)
            turned = swap(value)
            top = jnp.concatenate([jnp.where(low, value, 0.0), jnp.where(low, turned, 0.0)], axis=1)
            bottom = jnp.concatenate([jnp.where(low, 0.0, turned), jnp.where(low, 0.0, value)], axis=1)
            weight = jnp.concatenate([top.astype(jnp.bfloat16), bottom.astype(jnp.bfloat16)], axis=0)
            part = jnp.dot(left[b], weight, preferred_element_type=jnp.float32).astype(jnp.bfloat16)
            for g in range(depth // 2):
                for e in range(2):
                    mid[b, pl.ds((2 * pair + e) * VB, VB), g * LANES:(g + 1) * LANES] = (
                        part[g * VB:(g + 1) * VB, e * LANES:(e + 1) * LANES])
            for step in beside[pair * each:(pair + 1) * each]:
                step()
        total = lax.dot_general(
            mid[b], right[b], (((1,), (1,)), ((), ())), preferred_element_type=jnp.float32)
        total = total.reshape(rows, 2, HALF, LANES)
        total = jnp.where(low_half(HALF)[None], total[:, 0], total[:, 1])
        for r in range(reps):
            kept[s, r] = total[r * share:(r + 1) * share].reshape(share * HALF, LANES)

    def exchange(s):
        for i in range(1, reps):
            rs_send[s, i - 1] = kept[s, rep_peer(i)].astype(jnp.bfloat16)
            rs_copy(s, i).start()

    def summed(s):
        total = kept[s, my_rep]
        for i in range(1, reps):
            rs_copy(s, i).wait_recv()
            total = total + rs_recv[s, i - 1].astype(jnp.float32)
        return total.astype(jnp.bfloat16)

    def finish(s):
        back[s] = summed(s)
        back_copy(s).start()

    loads[4].wait()
    for k in range(tiles):
        for r in range(share):
            coup = coup_ref[my_rep * share + r].astype(jnp.float32)
            chosen = lax.broadcasted_iota(jnp.int32, coup.shape, 1) == blocks_ref[0, k]
            coup = jnp.sum(jnp.where(chosen, coup, 0.0), axis=1, keepdims=True)
            terms = jnp.zeros((HALF, LANES), jnp.float32)
            for p in range(rows):
                terms = terms + coup[p:p + 1] * wide[k, pl.ds(p, HALF, stride=rows), :]
            cyc[k, pl.ds(r * HALF, HALF), :] = terms

    loads[5].wait()
    for step in prepare(0, own_tags[0]):
        step()

    @pl.loop(1, peers)
    def _(o):
        tag_copy(o).wait_recv()
        to_smem(o).start()

    @pl.loop(1, peers)
    def _(o):
        to_smem(o).wait()

    @pl.loop(0, steps)
    def _(n):
        s0 = jnp.where(n == 0, 0, 2 * n + 1)
        s1 = jnp.where(n == steps - 1, 1, 2 * n + 2)
        s2 = jnp.where(n == steps - 1, CAP, 2 * n + 3)
        tag1 = jnp.where(n == steps - 1, own_tags[1], tag_smem[jnp.maximum(s1 // CAP, 1), s1 % CAP, 0])
        tag2 = tag_smem[s2 // CAP, s2 % CAP, 0]

        @pl.when(n > 0)
        def _():
            x_copy(s0).wait_recv()

        compute(0, s0, prepare(1, tag1))
        exchange(s0)

        @pl.when(n > 0)
        def _():
            finish(2 * n)

        @pl.when(n < steps - 1)
        def _():
            x_copy(s1).wait_recv()

        compute(1, s1, prepare(0, tag2))
        exchange(s1)

        @pl.when(n > 0)
        def _():
            finish(s0)

    for j in range(CAP):
        ret[j] = summed(j)

    @pl.loop(CAP, slots)
    def _(s):
        back_copy(s).wait_recv()

    for k in range(tiles):
        wide[k, pl.ds(0, share * HALF), :] = ret[slot[k]].astype(jnp.float32) + cyc[k]
    for k in range(tiles):
        for j in range(HALF):
            part = wide[k, pl.ds(j, share, stride=HALF), :]
            out_ref[k, :, j * LANES:(j + 1) * LANES] = part.astype(out_ref.dtype)

    @pl.loop(1, peers)
    def _(o):
        tag_copy(o).wait_send()

    @pl.loop(CAP, slots)
    def _(s):
        x_copy(s).wait_send()
        back_copy(s).wait_send()

    @pl.loop(0, slots)
    def _(s):
        for i in range(1, reps):
            rs_copy(s, i).wait_send()


def solution(mesh):
    peers, reps = mesh.shape["tile"], mesh.shape["rep"]

    def local(amplitudes, tile_blocks, live_rows, ladder_factors, cycle_coupling, block_owner):
        tiles, rows, cells = amplitudes.shape
        owned, _, depth, _ = ladder_factors.shape
        share = rows // reps
        slots = peers * CAP
        bf16, f32, dma = jnp.bfloat16, jnp.float32, pltpu.SemaphoreType.DMA
        smem, vmem = pltpu.SMEM, pltpu.VMEM
        return pl.pallas_call(
            functools.partial(kernel, peers, reps, tiles, depth, share, rows),
            out_shape=jax.ShapeDtypeStruct((tiles, share, cells), bf16),
            in_specs=[pl.BlockSpec(memory_space=pl.ANY)] * 6,
            out_specs=pl.BlockSpec(memory_space=vmem),
            scratch_shapes=[
                smem(tile_blocks.shape[::-1], jnp.int32),
                smem(live_rows.shape, jnp.int32),
                smem(block_owner.shape, jnp.int32),
                vmem(amplitudes.shape, bf16),
                vmem((rows, rows, cycle_coupling.shape[0]), bf16),
                vmem(ladder_factors.shape, bf16),
                vmem((tiles, rows * HALF, LANES), f32),
                vmem((4, depth * HALF, LANES), f32),
                vmem((tiles, rows // 2 * VB, LANES), f32),
                vmem((4 * VB, LANES), f32),
                vmem((tiles, rows // 2 * VB, LANES), bf16),
                vmem((slots, rows // 2 * VB, LANES), bf16),
                vmem((slots, rows // 2 * VB, LANES), bf16),
                vmem((peers, 8, LANES), jnp.int32),
                vmem((peers, 8, LANES), jnp.int32),
                smem((peers, 8, LANES), jnp.int32),
                vmem((2, depth // 2 * VB, LANES), bf16),
                vmem((2, LANES, depth * VB), bf16),
                vmem((2, rows * VB, depth * VB), bf16),
                vmem((slots, reps, share * HALF, LANES), f32),
                vmem((slots, reps - 1, share * HALF, LANES), bf16),
                vmem((slots, reps - 1, share * HALF, LANES), bf16),
                vmem((slots, share * HALF, LANES), bf16),
                vmem((slots, share * HALF, LANES), bf16),
                vmem((tiles, share * HALF, LANES), f32),
                dma((6,)),
                dma((peers,)),
                dma((peers,)),
                dma((peers,)),
                dma((slots,)),
                dma((slots,)),
                dma((slots, reps - 1)),
                dma((slots, reps - 1)),
                dma((slots,)),
                dma((slots,)),
            ],
            compiler_params=pltpu.CompilerParams(
                collective_id=0, has_side_effects=True, vmem_limit_bytes=62 * 2**20
            ),
            name="ladder",
        )(
            tile_blocks.T, live_rows, block_owner, amplitudes,
            jnp.transpose(cycle_coupling, (1, 2, 0)), ladder_factors)

    placed = (
        P(("grp", "tile"), None, None),
        P(("grp", "tile"), None),
        P(("grp", "tile")),
        P("tile", None, "rep", None),
        P(),
        P(),
    )
    return jax.shard_map(
        local,
        mesh=mesh,
        in_specs=placed,
        out_specs=P(("grp", "tile"), "rep", None),
        check_vma=False,
    )
```

```python
import functools

import jax
import jax.numpy as jnp
from jax import lax
from jax.experimental import pallas as pl
from jax.experimental.pallas import tpu as pltpu
from jax.sharding import PartitionSpec as P

VB = 64
CAP = 2
LANES = 128
HALF = VB // 2
MESH = pl.DeviceIdType.MESH


def low_half(rows):
    return lax.broadcasted_iota(jnp.int32, (rows, LANES), 1) < VB


def swap(value):
    return pltpu.roll(value, VB, 1)


def pair_rows(first, second):
    low = low_half(first.shape[0])
    even = jnp.where(low, first, swap(second))
    odd = jnp.where(low, swap(first), second)
    return even, odd


def spread_rows(value, wide):
    n = value.shape[0]
    for j in range(HALF):
        wide[pl.ds(j * n, n), :] = value[:, j * LANES:(j + 1) * LANES]


def kernel(
    peers, reps, tiles, depth, share, rows,
    blocks_hbm, live_hbm, owner_hbm, amp_hbm, coup_hbm, fac_hbm,
    out_ref,
    blocks_ref, live_ref, owner_ref, amp_ref, coup_ref, fac, wide, cwide, native, order, xtile, ctile, packed, xs, xr,
    tag_send, tag_recv, tag_smem, left, right, mid, kept, rs_send, rs_recv, back, ret, cyc,
    in_sem, tag_local, tag_ssem, tag_rsem, x_ssem, x_rsem, rs_ssem, rs_rsem, b_ssem, b_rsem,
):
    chips = peers // 2
    slots = peers * CAP
    steps = slots // 2
    owned = fac_hbm.shape[0]
    me = lax.axis_index("tile")
    my_rep = lax.axis_index("rep")
    my_chip, my_core = me // 2, me % 2

    def to_peer(o):
        return (my_chip + o // 2) % chips * 2 + (my_core + o % 2) % 2

    def from_peer(o):
        return (my_chip + chips - o // 2) % chips * 2 + (my_core + o % 2) % 2

    def rep_peer(i):
        return (my_rep + i) % reps

    loads = [
        pltpu.make_async_copy(source, target, in_sem.at[n])
        for n, (source, target) in enumerate((
            (amp_hbm, amp_ref), (blocks_hbm, blocks_ref), (live_hbm, live_ref),
            (owner_hbm, owner_ref), (coup_hbm, coup_ref), (fac_hbm, fac)))
    ]
    for load in loads:
        load.start()

    barrier = pltpu.get_barrier_semaphore()

    @pl.loop(1, peers)
    def _(o):
        pl.semaphore_signal(barrier, inc=1, device_id={"tile": to_peer(o)}, device_id_type=MESH)

    for i in range(1, reps):
        pl.semaphore_signal(barrier, inc=1, device_id={"rep": rep_peer(i)}, device_id_type=MESH)

    for load in loads[1:4]:
        load.wait()

    target, within, slot = [], [], []
    for k in range(tiles):
        place = owner_ref[blocks_ref[1, k]]
        t = place // owned
        rank = 0
        for e in range(k):
            rank = rank + jnp.where(target[e] == t, 1, 0)
        m = (t // 2 + chips - my_chip) % chips
        c = (t % 2 + 2 - my_core) % 2
        target.append(t)
        within.append(place - t * owned)
        slot.append((m * 2 + c) * CAP + jnp.minimum(rank, CAP - 1))

    def in_slot(s):
        pick, tag = 0, 0
        for k in range(tiles):
            hit = slot[k] == s
            pick = jnp.where(hit, k, pick)
            tag = jnp.where(hit, within[k], tag)
        return pick, tag

    loads[0].wait()

    row = lax.broadcasted_iota(jnp.int32, (rows, VB * VB), 0)
    for k in range(tiles):
        masked = jnp.where(row < live_ref[k], amp_ref[k].astype(jnp.float32), 0.0)
        spread_rows(masked, wide.at[k])
    for k in range(tiles):
        for pair in range(rows // 2):
            first = wide[k, pl.ds(2 * pair, HALF, stride=rows), :]
            second = wide[k, pl.ds(2 * pair + 1, HALF, stride=rows), :]
            even, odd = pair_rows(first, second)
            xtile[k, pl.ds(pair * VB, HALF, stride=2), :] = even
            xtile[k, pl.ds(pair * VB + 1, HALF, stride=2), :] = odd
    for k in range(tiles):
        packed[k] = xtile[k].astype(jnp.bfloat16)

    own_tags = []
    for j in range(CAP):
        pick, tag = in_slot(j)
        xr[j] = packed[pick]
        own_tags.append(tag)

    @pl.loop(1, peers)
    def _(o):
        tags = jnp.zeros((8, LANES), jnp.int32)
        row = lax.broadcasted_iota(jnp.int32, (8, LANES), 0)
        for j in range(CAP):
            pick, tag = in_slot(o * CAP + j)
            tags = jnp.where(row == j, tag, tags)
            xs[o * CAP + j] = packed[pick]
        tag_send[o] = tags

    pl.semaphore_wait(barrier, peers - 1 + reps - 1)

    def tag_copy(o):
        return pltpu.make_async_remote_copy(
            src_ref=tag_send.at[o], dst_ref=tag_recv.at[o], send_sem=tag_ssem.at[o], recv_sem=tag_rsem.at[o],
            device_id={"tile": to_peer(o)}, device_id_type=MESH)

    def x_copy(s):
        return pltpu.make_async_remote_copy(
            src_ref=xs.at[s], dst_ref=xr.at[s], send_sem=x_ssem.at[s], recv_sem=x_rsem.at[s],
            device_id={"tile": to_peer(s // CAP)}, device_id_type=MESH)

    def rs_copy(s, i):
        return pltpu.make_async_remote_copy(
            src_ref=rs_send.at[s, i - 1], dst_ref=rs_recv.at[s, i - 1],
            send_sem=rs_ssem.at[s, i - 1], recv_sem=rs_rsem.at[s, i - 1],
            device_id={"rep": rep_peer(i)}, device_id_type=MESH)

    def back_copy(s):
        return pltpu.make_async_remote_copy(
            src_ref=back.at[s], dst_ref=ret.at[s], send_sem=b_ssem.at[s], recv_sem=b_rsem.at[s],
            device_id={"tile": from_peer(s // CAP)}, device_id_type=MESH)

    def to_smem(o):
        return pltpu.make_async_copy(tag_recv.at[o], tag_smem.at[o], tag_local.at[o])

    @pl.loop(1, peers)
    def _(o):
        tag_copy(o).start()

    @pl.loop(2 * CAP, slots)
    def _(s):
        x_copy(s).start()

    for s in range(CAP, 2 * CAP):
        x_copy(s).start()

    low = low_half(VB)
    span = depth * HALF // 2
    to = lax.broadcasted_iota(jnp.int32, order.shape, 0)
    at = lax.broadcasted_iota(jnp.int32, order.shape, 1)
    order[...] = jnp.where(at == (to % HALF) * depth + to // HALF, 1.0, 0.0).astype(jnp.bfloat16)

    def prepare(b, block):
        def natural():
            for j in range(HALF):
                for side in range(2):
                    native[b, pl.ds(j * depth, depth), side * LANES:(side + 1) * LANES] = (
                        fac[block, side, :, j * LANES:(j + 1) * LANES])

        def turn(half):
            some = pl.ds(half * span, span)
            cwide[b, some, :] = jnp.dot(order[some, :], native[b], preferred_element_type=jnp.float32)

        def both(pair):
            first = cwide[b, pl.ds(2 * pair * HALF, HALF), 0:LANES]
            second = cwide[b, pl.ds((2 * pair + 1) * HALF, HALF), 0:LANES]
            even, odd = pair_rows(first, second)
            left[b, pl.ds(pair * VB, HALF), :] = even.astype(jnp.bfloat16)
            left[b, pl.ds(pair * VB + HALF, HALF), :] = odd.astype(jnp.bfloat16)
            first = cwide[b, pl.ds(2 * pair * HALF, HALF), LANES:]
            second = cwide[b, pl.ds((2 * pair + 1) * HALF, HALF), LANES:]
            even, odd = pair_rows(first, second)
            ctile[pl.ds(pair % 4 * VB, HALF, stride=2), :] = even
            ctile[pl.ds(pair % 4 * VB + 1, HALF, stride=2), :] = odd
            value = ctile[pl.ds(pair % 4 * VB, VB), :].astype(jnp.bfloat16)
            right[b, 0:VB, pair * LANES:(pair + 1) * LANES] = value
            right[b, VB:, pair * LANES:(pair + 1) * LANES] = value

        steps = [natural]
        for half in range(2):
            steps.append(functools.partial(turn, half))
            steps += [functools.partial(both, pair) for pair in range(half * depth // 4, (half + 1) * depth // 4)]
        return steps

    def compute(b, s, beside):
        message = xr.at[s]
        each = -(-len(beside) // (rows // 2))
        for pair in range(rows // 2):
            value = message[pl.ds(pair * VB, VB), :].astype(jnp.float32)
            turned = swap(value)
            top = jnp.concatenate([jnp.where(low, value, 0.0), jnp.where(low, turned, 0.0)], axis=1)
            bottom = jnp.concatenate([jnp.where(low, 0.0, turned), jnp.where(low, 0.0, value)], axis=1)
            weight = jnp.concatenate([top.astype(jnp.bfloat16), bottom.astype(jnp.bfloat16)], axis=0)
            part = jnp.dot(left[b], weight, preferred_element_type=jnp.float32).astype(jnp.bfloat16)
            for g in range(depth // 2):
                for e in range(2):
                    mid[b, pl.ds((2 * pair + e) * VB, VB), g * LANES:(g + 1) * LANES] = (
                        part[g * VB:(g + 1) * VB, e * LANES:(e + 1) * LANES])
            for step in beside[pair * each:(pair + 1) * each]:
                step()
        total = lax.dot_general(
            mid[b], right[b], (((1,), (1,)), ((), ())), preferred_element_type=jnp.float32)
        total = total.reshape(rows, 2, HALF, LANES)
        total = jnp.where(low_half(HALF)[None], total[:, 0], total[:, 1])
        for r in range(reps):
            kept[s, r] = total[r * share:(r + 1) * share].reshape(share * HALF, LANES)

    def exchange(s):
        for i in range(1, reps):
            rs_send[s, i - 1] = kept[s, rep_peer(i)].astype(jnp.bfloat16)
            rs_copy(s, i).start()

    def summed(s):
        total = kept[s, my_rep]
        for i in range(1, reps):
            rs_copy(s, i).wait_recv()
            total = total + rs_recv[s, i - 1].astype(jnp.float32)
        return total.astype(jnp.bfloat16)

    def finish(s):
        back[s] = summed(s)
        back_copy(s).start()

    loads[4].wait()
    for k in range(tiles):
        for r in range(share):
            coup = coup_ref[my_rep * share + r].astype(jnp.float32)
            chosen = lax.broadcasted_iota(jnp.int32, coup.shape, 1) == blocks_ref[0, k]
            coup = jnp.sum(jnp.where(chosen, coup, 0.0), axis=1, keepdims=True)
            terms = jnp.zeros((HALF, LANES), jnp.float32)
            for p in range(rows):
                terms = terms + coup[p:p + 1] * wide[k, pl.ds(p, HALF, stride=rows), :]
            cyc[k, pl.ds(r * HALF, HALF), :] = terms

    loads[5].wait()
    for step in prepare(0, own_tags[0]):
        step()

    @pl.loop(1, peers)
    def _(o):
        tag_copy(o).wait_recv()
        to_smem(o).start()

    @pl.loop(1, peers)
    def _(o):
        to_smem(o).wait()

    @pl.loop(0, steps)
    def _(n):
        s0 = jnp.where(n == 0, 0, 2 * n + 1)
        s1 = jnp.where(n == steps - 1, 1, 2 * n + 2)
        s2 = jnp.where(n == steps - 1, CAP, 2 * n + 3)
        tag1 = jnp.where(n == steps - 1, own_tags[1], tag_smem[jnp.maximum(s1 // CAP, 1), s1 % CAP, 0])
        tag2 = tag_smem[s2 // CAP, s2 % CAP, 0]

        @pl.when(n > 0)
        def _():
            x_copy(s0).wait_recv()

        compute(0, s0, prepare(1, tag1))
        exchange(s0)

        @pl.when(n > 0)
        def _():
            finish(2 * n)

        @pl.when(n < steps - 1)
        def _():
            x_copy(s1).wait_recv()

        compute(1, s1, prepare(0, tag2))
        exchange(s1)

        @pl.when(n > 0)
        def _():
            finish(s0)

    for j in range(CAP):
        ret[j] = summed(j)

    @pl.loop(CAP, slots)
    def _(s):
        back_copy(s).wait_recv()

    for k in range(tiles):
        wide[k, pl.ds(0, share * HALF), :] = ret[slot[k]].astype(jnp.float32) + cyc[k]
    for k in range(tiles):
        for j in range(HALF):
            part = wide[k, pl.ds(j, share, stride=HALF), :]
            out_ref[k, :, j * LANES:(j + 1) * LANES] = part.astype(out_ref.dtype)

    @pl.loop(1, peers)
    def _(o):
        tag_copy(o).wait_send()

    @pl.loop(CAP, slots)
    def _(s):
        x_copy(s).wait_send()
        back_copy(s).wait_send()

    @pl.loop(0, slots)
    def _(s):
        for i in range(1, reps):
            rs_copy(s, i).wait_send()


def solution(mesh):
    peers, reps = mesh.shape["tile"], mesh.shape["rep"]

    def local(amplitudes, tile_blocks, live_rows, ladder_factors, cycle_coupling, block_owner):
        tiles, rows, cells = amplitudes.shape
        owned, _, depth, _ = ladder_factors.shape
        share = rows // reps
        slots = peers * CAP
        bf16, f32, dma = jnp.bfloat16, jnp.float32, pltpu.SemaphoreType.DMA
        smem, vmem = pltpu.SMEM, pltpu.VMEM
        return pl.pallas_call(
            functools.partial(kernel, peers, reps, tiles, depth, share, rows),
            out_shape=jax.ShapeDtypeStruct((tiles, share, cells), bf16),
            in_specs=[pl.BlockSpec(memory_space=pl.ANY)] * 6,
            out_specs=pl.BlockSpec(memory_space=vmem),
            scratch_shapes=[
                smem(tile_blocks.shape[::-1], jnp.int32),
                smem(live_rows.shape, jnp.int32),
                smem(block_owner.shape, jnp.int32),
                vmem(amplitudes.shape, bf16),
                vmem((rows, rows, cycle_coupling.shape[0]), bf16),
                vmem(ladder_factors.shape, bf16),
                vmem((tiles, rows * HALF, LANES), f32),
                vmem((2, depth * HALF, 2 * LANES), f32),
                vmem((2, depth * HALF, 2 * LANES), bf16),
                vmem((depth * HALF, depth * HALF), bf16),
                vmem((tiles, rows // 2 * VB, LANES), f32),
                vmem((4 * VB, LANES), f32),
                vmem((tiles, rows // 2 * VB, LANES), bf16),
                vmem((slots, rows // 2 * VB, LANES), bf16),
                vmem((slots, rows // 2 * VB, LANES), bf16),
                vmem((peers, 8, LANES), jnp.int32),
                vmem((peers, 8, LANES), jnp.int32),
                smem((peers, 8, LANES), jnp.int32),
                vmem((2, depth // 2 * VB, LANES), bf16),
                vmem((2, LANES, depth * VB), bf16),
                vmem((2, rows * VB, depth * VB), bf16),
                vmem((slots, reps, share * HALF, LANES), f32),
                vmem((slots, reps - 1, share * HALF, LANES), bf16),
                vmem((slots, reps - 1, share * HALF, LANES), bf16),
                vmem((slots, share * HALF, LANES), bf16),
                vmem((slots, share * HALF, LANES), bf16),
                vmem((tiles, share * HALF, LANES), f32),
                dma((6,)),
                dma((peers,)),
                dma((peers,)),
                dma((peers,)),
                dma((slots,)),
                dma((slots,)),
                dma((slots, reps - 1)),
                dma((slots, reps - 1)),
                dma((slots,)),
                dma((slots,)),
            ],
            compiler_params=pltpu.CompilerParams(
                collective_id=0, has_side_effects=True, vmem_limit_bytes=62 * 2**20
            ),
            name="ladder",
        )(
            tile_blocks.T, live_rows, block_owner, amplitudes,
            jnp.transpose(cycle_coupling, (1, 2, 0)), ladder_factors)

    placed = (
        P(("grp", "tile"), None, None),
        P(("grp", "tile"), None),
        P(("grp", "tile")),
        P("tile", None, "rep", None),
        P(),
        P(),
    )
    return jax.shard_map(
        local,
        mesh=mesh,
        in_specs=placed,
        out_specs=P(("grp", "tile"), "rep", None),
        check_vma=False,
    )
```

```python
import functools

import jax
import jax.numpy as jnp
from jax import lax
from jax.experimental import pallas as pl
from jax.experimental.pallas import tpu as pltpu
from jax.sharding import PartitionSpec as P

VB = 64
CAP = 2
LANES = 128
HALF = VB // 2
MESH = pl.DeviceIdType.MESH


def low_half(rows):
    return lax.broadcasted_iota(jnp.int32, (rows, LANES), 1) < VB


def swap(value):
    return pltpu.roll(value, VB, 1)


def pair_rows(first, second):
    low = low_half(first.shape[0])
    even = jnp.where(low, first, swap(second))
    odd = jnp.where(low, swap(first), second)
    return even, odd


def spread_rows(value, wide):
    n = value.shape[0]
    for j in range(HALF):
        wide[pl.ds(j * n, n), :] = value[:, j * LANES:(j + 1) * LANES]


def kernel(
    peers, reps, tiles, depth, share, rows,
    blocks_hbm, live_hbm, owner_hbm, amp_hbm, coup_hbm, fac_hbm,
    out_ref,
    blocks_ref, live_ref, owner_ref, amp_ref, coup_ref, fac, wide, cwide, xtile, ctile, packed, xs, xr,
    tag_send, tag_recv, tag_smem, left, right, mid, kept, back, ret, cyc,
    in_sem, tag_local, tag_ssem, tag_rsem, x_ssem, x_rsem, b_ssem, b_rsem,
):
    chips = peers // 2
    slots = peers * CAP
    steps = slots // 2
    owned = fac_hbm.shape[0]
    me = lax.axis_index("tile")
    my_rep = lax.axis_index("rep")
    my_chip, my_core = me // 2, me % 2

    def to_peer(o):
        return (my_chip + o // 2) % chips * 2 + (my_core + o % 2) % 2

    def from_peer(o):
        return (my_chip + chips - o // 2) % chips * 2 + (my_core + o % 2) % 2

    def rep_peer(i):
        return (my_rep + i) % reps

    loads = [
        pltpu.make_async_copy(source, target, in_sem.at[n])
        for n, (source, target) in enumerate((
            (amp_hbm, amp_ref), (blocks_hbm, blocks_ref), (live_hbm, live_ref),
            (owner_hbm, owner_ref), (coup_hbm, coup_ref), (fac_hbm, fac)))
    ]
    for load in loads:
        load.start()

    barrier = pltpu.get_barrier_semaphore()

    for i in range(reps):
        @pl.loop(0 if i else 1, peers)
        def _(o):
            pl.semaphore_signal(
                barrier, inc=1, device_id={"tile": to_peer(o), "rep": rep_peer(i)}, device_id_type=MESH)

    for load in loads[1:4]:
        load.wait()

    target, within, slot = [], [], []
    for k in range(tiles):
        place = owner_ref[blocks_ref[1, k]]
        t = place // owned
        rank = 0
        for e in range(k):
            rank = rank + jnp.where(target[e] == t, 1, 0)
        m = (t // 2 + chips - my_chip) % chips
        c = (t % 2 + 2 - my_core) % 2
        target.append(t)
        within.append(place - t * owned)
        slot.append((m * 2 + c) * CAP + jnp.minimum(rank, CAP - 1))

    def in_slot(s):
        pick, tag = 0, 0
        for k in range(tiles):
            hit = slot[k] == s
            pick = jnp.where(hit, k, pick)
            tag = jnp.where(hit, within[k], tag)
        return pick, tag

    loads[0].wait()

    row = lax.broadcasted_iota(jnp.int32, (rows, VB * VB), 0)
    for k in range(tiles):
        masked = jnp.where(row < live_ref[k], amp_ref[k].astype(jnp.float32), 0.0)
        spread_rows(masked, wide.at[k])
    for k in range(tiles):
        for pair in range(rows // 2):
            first = wide[k, pl.ds(2 * pair, HALF, stride=rows), :]
            second = wide[k, pl.ds(2 * pair + 1, HALF, stride=rows), :]
            even, odd = pair_rows(first, second)
            xtile[k, pl.ds(pair * VB, HALF, stride=2), :] = even
            xtile[k, pl.ds(pair * VB + 1, HALF, stride=2), :] = odd
    for k in range(tiles):
        packed[k] = xtile[k].astype(jnp.bfloat16)

    own_tags = []
    for j in range(CAP):
        pick, tag = in_slot(j)
        xr[j] = packed[pick]
        own_tags.append(tag)

    @pl.loop(1, peers)
    def _(o):
        tags = jnp.zeros((8, LANES), jnp.int32)
        row = lax.broadcasted_iota(jnp.int32, (8, LANES), 0)
        for j in range(CAP):
            pick, tag = in_slot(o * CAP + j)
            tags = jnp.where(row == j, tag, tags)
            xs[o * CAP + j] = packed[pick]
        tag_send[o] = tags

    pl.semaphore_wait(barrier, peers * reps - 1)

    def tag_copy(o):
        return pltpu.make_async_remote_copy(
            src_ref=tag_send.at[o], dst_ref=tag_recv.at[o], send_sem=tag_ssem.at[o], recv_sem=tag_rsem.at[o],
            device_id={"tile": to_peer(o)}, device_id_type=MESH)

    def x_copy(s):
        return pltpu.make_async_remote_copy(
            src_ref=xs.at[s], dst_ref=xr.at[s], send_sem=x_ssem.at[s], recv_sem=x_rsem.at[s],
            device_id={"tile": to_peer(s // CAP)}, device_id_type=MESH)

    def back_copy(s, i):
        return pltpu.make_async_remote_copy(
            src_ref=back.at[s, i], dst_ref=ret.at[s, i], send_sem=b_ssem.at[s, i], recv_sem=b_rsem.at[s, i],
            device_id={"tile": from_peer(s // CAP), "rep": rep_peer(i)}, device_id_type=MESH)

    def to_smem(o):
        return pltpu.make_async_copy(tag_recv.at[o], tag_smem.at[o], tag_local.at[o])

    @pl.loop(1, peers)
    def _(o):
        tag_copy(o).start()

    @pl.loop(2 * CAP, slots)
    def _(s):
        x_copy(s).start()

    for s in range(CAP, 2 * CAP):
        x_copy(s).start()

    low = low_half(VB)

    def prepare(b, block):
        def spread():
            spread_rows(fac[block, 0].astype(jnp.float32), cwide.at[2 * b])
            spread_rows(fac[block, 1].astype(jnp.float32), cwide.at[2 * b + 1])

        def both(pair):
            first = cwide[2 * b, pl.ds(2 * pair, HALF, stride=depth), :]
            second = cwide[2 * b, pl.ds(2 * pair + 1, HALF, stride=depth), :]
            even, odd = pair_rows(first, second)
            left[b, pl.ds(pair * VB, HALF), :] = even.astype(jnp.bfloat16)
            left[b, pl.ds(pair * VB + HALF, HALF), :] = odd.astype(jnp.bfloat16)
            first = cwide[2 * b + 1, pl.ds(2 * pair, HALF, stride=depth), :]
            second = cwide[2 * b + 1, pl.ds(2 * pair + 1, HALF, stride=depth), :]
            even, odd = pair_rows(first, second)
            ctile[pl.ds(pair % 4 * VB, HALF, stride=2), :] = even
            ctile[pl.ds(pair % 4 * VB + 1, HALF, stride=2), :] = odd
            value = ctile[pl.ds(pair % 4 * VB, VB), :].astype(jnp.bfloat16)
            right[b, 0:VB, pair * LANES:(pair + 1) * LANES] = value
            right[b, VB:, pair * LANES:(pair + 1) * LANES] = value

        return [spread] + [functools.partial(both, pair) for pair in range(depth // 2)]

    def compute(b, s, beside):
        message = xr.at[s]
        each = -(-len(beside) // (rows // 2))
        for pair in range(rows // 2):
            value = message[pl.ds(pair * VB, VB), :].astype(jnp.float32)
            turned = swap(value)
            top = jnp.concatenate([jnp.where(low, value, 0.0), jnp.where(low, turned, 0.0)], axis=1)
            bottom = jnp.concatenate([jnp.where(low, 0.0, turned), jnp.where(low, 0.0, value)], axis=1)
            weight = jnp.concatenate([top.astype(jnp.bfloat16), bottom.astype(jnp.bfloat16)], axis=0)
            part = jnp.dot(left[b], weight, preferred_element_type=jnp.float32).astype(jnp.bfloat16)
            for g in range(depth // 2):
                for e in range(2):
                    mid[b, pl.ds((2 * pair + e) * VB, VB), g * LANES:(g + 1) * LANES] = (
                        part[g * VB:(g + 1) * VB, e * LANES:(e + 1) * LANES])
            for step in beside[pair * each:(pair + 1) * each]:
                step()
        total = lax.dot_general(
            mid[b], right[b], (((1,), (1,)), ((), ())), preferred_element_type=jnp.float32)
        total = total.reshape(rows, 2, HALF, LANES)
        total = jnp.where(low_half(HALF)[None], total[:, 0], total[:, 1])
        for r in range(reps):
            kept[s, r] = total[r * share:(r + 1) * share].reshape(share * HALF, LANES)

    def send(s):
        for i in range(reps):
            back[s, i] = kept[s, rep_peer(i)].astype(jnp.bfloat16)
        for i in range(1, reps):
            back_copy(s, i).start()

        @pl.when(s >= CAP)
        def _():
            back_copy(s, 0).start()

    loads[4].wait()
    for k in range(tiles):
        for r in range(share):
            coup = coup_ref[my_rep * share + r].astype(jnp.float32)
            chosen = lax.broadcasted_iota(jnp.int32, coup.shape, 1) == blocks_ref[0, k]
            coup = jnp.sum(jnp.where(chosen, coup, 0.0), axis=1, keepdims=True)
            terms = jnp.zeros((HALF, LANES), jnp.float32)
            for p in range(rows):
                terms = terms + coup[p:p + 1] * wide[k, pl.ds(p, HALF, stride=rows), :]
            cyc[k, pl.ds(r * HALF, HALF), :] = terms

    loads[5].wait()
    for step in prepare(0, own_tags[0]):
        step()

    @pl.loop(1, peers)
    def _(o):
        tag_copy(o).wait_recv()
        to_smem(o).start()

    @pl.loop(1, peers)
    def _(o):
        to_smem(o).wait()

    @pl.loop(0, steps)
    def _(n):
        s0 = jnp.where(n == 0, 0, 2 * n + 1)
        s1 = jnp.where(n == steps - 1, 1, 2 * n + 2)
        s2 = jnp.where(n == steps - 1, CAP, 2 * n + 3)
        tag1 = jnp.where(n == steps - 1, own_tags[1], tag_smem[jnp.maximum(s1 // CAP, 1), s1 % CAP, 0])
        tag2 = tag_smem[s2 // CAP, s2 % CAP, 0]

        @pl.when(n > 0)
        def _():
            x_copy(s0).wait_recv()

        compute(0, s0, prepare(1, tag1))
        send(s0)

        @pl.when(n < steps - 1)
        def _():
            x_copy(s1).wait_recv()

        compute(1, s1, prepare(0, tag2))
        send(s1)

    for j in range(CAP):
        ret[j, 0] = back[j, 0]
        for i in range(1, reps):
            back_copy(j, i).wait_recv()

    @pl.loop(CAP, slots)
    def _(s):
        for i in range(reps):
            back_copy(s, i).wait_recv()

    for k in range(tiles):
        wide[k, pl.ds(0, share * HALF), :] = jnp.sum(ret[slot[k]].astype(jnp.float32), axis=0) + cyc[k]
    for k in range(tiles):
        for j in range(HALF):
            part = wide[k, pl.ds(j, share, stride=HALF), :]
            out_ref[k, :, j * LANES:(j + 1) * LANES] = part.astype(out_ref.dtype)

    @pl.loop(1, peers)
    def _(o):
        tag_copy(o).wait_send()

    @pl.loop(CAP, slots)
    def _(s):
        x_copy(s).wait_send()
        back_copy(s, 0).wait_send()

    @pl.loop(0, slots)
    def _(s):
        for i in range(1, reps):
            back_copy(s, i).wait_send()


def solution(mesh):
    peers, reps = mesh.shape["tile"], mesh.shape["rep"]

    def local(amplitudes, tile_blocks, live_rows, ladder_factors, cycle_coupling, block_owner):
        tiles, rows, cells = amplitudes.shape
        owned, _, depth, _ = ladder_factors.shape
        share = rows // reps
        slots = peers * CAP
        bf16, f32, dma = jnp.bfloat16, jnp.float32, pltpu.SemaphoreType.DMA
        smem, vmem = pltpu.SMEM, pltpu.VMEM
        return pl.pallas_call(
            functools.partial(kernel, peers, reps, tiles, depth, share, rows),
            out_shape=jax.ShapeDtypeStruct((tiles, share, cells), bf16),
            in_specs=[pl.BlockSpec(memory_space=pl.ANY)] * 6,
            out_specs=pl.BlockSpec(memory_space=vmem),
            scratch_shapes=[
                smem(tile_blocks.shape[::-1], jnp.int32),
                smem(live_rows.shape, jnp.int32),
                smem(block_owner.shape, jnp.int32),
                vmem(amplitudes.shape, bf16),
                vmem((rows, rows, cycle_coupling.shape[0]), bf16),
                vmem(ladder_factors.shape, bf16),
                vmem((tiles, rows * HALF, LANES), f32),
                vmem((4, depth * HALF, LANES), f32),
                vmem((tiles, rows // 2 * VB, LANES), f32),
                vmem((4 * VB, LANES), f32),
                vmem((tiles, rows // 2 * VB, LANES), bf16),
                vmem((slots, rows // 2 * VB, LANES), bf16),
                vmem((slots, rows // 2 * VB, LANES), bf16),
                vmem((peers, 8, LANES), jnp.int32),
                vmem((peers, 8, LANES), jnp.int32),
                smem((peers, 8, LANES), jnp.int32),
                vmem((2, depth // 2 * VB, LANES), bf16),
                vmem((2, LANES, depth * VB), bf16),
                vmem((2, rows * VB, depth * VB), bf16),
                vmem((slots, reps, share * HALF, LANES), f32),
                vmem((slots, reps, share * HALF, LANES), bf16),
                vmem((slots, reps, share * HALF, LANES), bf16),
                vmem((tiles, share * HALF, LANES), f32),
                dma((6,)),
                dma((peers,)),
                dma((peers,)),
                dma((peers,)),
                dma((slots,)),
                dma((slots,)),
                dma((slots, reps)),
                dma((slots, reps)),
            ],
            compiler_params=pltpu.CompilerParams(
                collective_id=0, has_side_effects=True, vmem_limit_bytes=62 * 2**20
            ),
            name="ladder",
        )(
            tile_blocks.T, live_rows, block_owner, amplitudes,
            jnp.transpose(cycle_coupling, (1, 2, 0)), ladder_factors)

    placed = (
        P(("grp", "tile"), None, None),
        P(("grp", "tile"), None),
        P(("grp", "tile")),
        P("tile", None, "rep", None),
        P(),
        P(),
    )
    return jax.shard_map(
        local,
        mesh=mesh,
        in_specs=placed,
        out_specs=P(("grp", "tile"), "rep", None),
        check_vma=False,
    )
```
